256 devices in a mesh: dp: 32 (over x, y, core), ffn: 8 (over z).
Axes of the slice: x: 4, y: 4, z: 8, core: 2. Of those that a mesh axis runs over, the one named last changes fastest.
Arguments:
- resid: bfloat16 [1024, 8192], P('dp', 'ffn'), may hold values from -6 to 6
- attn_out: bfloat16 [1024, 8192], P('dp', 'ffn'), may hold values from -6 to 6
- norm_gain: float32 [8192], P('ffn'), may hold values from 0.25 to 1.75
- w_gate: bfloat16 [8192, 14784], P('ffn', 'dp'), may hold values from -0.0625 to 0.0625
- w_up: bfloat16 [8192, 14784], P('ffn', 'dp'), may hold values from -0.0625 to 0.0625
- w_down: bfloat16 [14784, 8192], P('dp', 'ffn'), may hold values from -0.046875 to 0.046875
- w_head: bfloat16 [8192, 18], P('ffn'), may hold values from -0.0625 to 0.0625
- actions: int32 [1024], P('dp'), may hold values from 0 to 17
- step_index: int32 [1024], P('dp'), may hold values from 0 to 63
- trace_code: int32 [1024], P('dp'), may hold values from 0 to 8
- targets: float32 [1024], P('dp'), may hold values from -6 to 6
Outputs:
- grad_gate: float32 [8192, 14784], P('ffn', 'dp')
- grad_up: float32 [8192, 14784], P('ffn', 'dp')
- grad_down: float32 [14784, 8192], P('dp', 'ffn')
- grad_head: float32 [8192, 18], P('ffn')
- loss: float32 [], replicated
The draws below stay inside these ranges and needn't reach their ends.
All inputs are finite; a program needn't handle non-finite values.
Results may differ from the reference program's by a relative error of at most 0.0062.
Values may be sent and summed in bfloat16 or wider, within the bound.
A program may use at most 64 MiB of HBM per device.

```python
import jax
import jax.numpy as jnp
from jax import lax

D = 8192
FF = 14784
ACTS = 18
HORIZON = 64
LEVELS = 8
TOKENS = 1024


def set_ends(values, own_key, low, top_value):
    index_at = [jax.random.randint(jax.random.fold_in(own_key, axis), (), 0, length) for axis, length in enumerate(values.shape)]
    widest = values.shape.index(max(values.shape))
    beside = index_at[:widest] + [(index_at[widest] + 1) % values.shape[widest]] + index_at[widest + 1:]
    return values.at[tuple(index_at)].set(low).at[tuple(beside)].set(top_value)


def block_levels(key, dims, split, least, top_value):
    loudness = 1.0
    for dim, blocks in split:
        draws = jax.random.uniform(jax.random.fold_in(jax.random.fold_in(key, 6), dim), (blocks,), jnp.float32, least / len(split), top_value / len(split))
        loudness = loudness * jnp.repeat(jnp.exp(draws), dims[dim] // blocks).reshape((-1,) + (1,) * (len(dims) - 1 - dim))
    return loudness


def scatter_about(key, extent, spread, most, cuts=(), held_as=jnp.bfloat16):
    result = spread * jax.random.normal(key, extent, jnp.float32)
    if cuts:
        result = result * block_levels(key, extent, cuts, -0.22, 0.18)
    return jnp.clip(result, -most, most).astype(held_as)


def setup_inputs(seed: int = 0) -> dict:
    key_list = jax.random.split(jax.random.key(seed), 12)
    return {
        "resid": scatter_about(key_list[0], (TOKENS, D), 1.0, 6.0, ((0, 32), (1, 8))),
        "attn_out": scatter_about(key_list[1], (TOKENS, D), 1.0, 6.0, ((0, 32), (1, 8))),
        "norm_gain": jnp.clip(1.0 + 0.15 * jax.random.normal(key_list[2], (D,), jnp.float32), 0.25, 1.75),
        "w_gate": scatter_about(key_list[3], (D, FF), D ** -0.5, 0.0625, ((0, 8), (1, 32))),
        "w_up": scatter_about(key_list[4], (D, FF), D ** -0.5, 0.0625, ((0, 8), (1, 32))),
        "w_down": scatter_about(key_list[5], (FF, D), FF ** -0.5, 0.046875, ((0, 32), (1, 8))),
        "w_head": scatter_about(key_list[6], (D, ACTS), D ** -0.5, 0.0625, ((0, 8),)),
        "actions": set_ends(jax.random.randint(key_list[7], (TOKENS,), 0, ACTS), jax.random.fold_in(key_list[7], 1), 0, ACTS - 1).astype(jnp.int32),
        "step_index": set_ends(jax.random.randint(key_list[8], (TOKENS,), 0, HORIZON), jax.random.fold_in(key_list[8], 1), 0, HORIZON - 1).astype(jnp.int32),
        "trace_code": set_ends(jax.random.randint(key_list[9], (TOKENS,), 0, LEVELS + 1), jax.random.fold_in(key_list[9], 1), 0, LEVELS).astype(jnp.int32),
        "targets": scatter_about(key_list[10], (TOKENS,), 1.0, 6.0, ((0, 32),), jnp.float32),
    }


def reference(resid, attn_out, norm_gain, w_gate, w_up, w_down, w_head, actions, step_index, trace_code, targets):
    summed = resid.astype(jnp.float32) + attn_out.astype(jnp.float32)
    normed = (summed * lax.rsqrt(lax.optimization_barrier(jnp.mean(summed * summed, axis=1, keepdims=True)) + 1e-06) * norm_gain).astype(jnp.bfloat16)
    gate = jnp.dot(normed, w_gate, preferred_element_type=jnp.float32)
    up_proj = jnp.dot(normed, w_up, preferred_element_type=jnp.float32)
    hidden = (jax.nn.silu(gate) * up_proj).astype(jnp.bfloat16)
    output = summed + jnp.dot(hidden, w_down, preferred_element_type=jnp.float32)
    critic_head = w_head.astype(jnp.float32)
    values = jnp.dot(output, critic_head, precision=lax.Precision.HIGHEST)
    one_hot = (actions[:, None] == jnp.arange(ACTS, dtype=jnp.int32)[None, :]).astype(jnp.float32)
    value = lax.optimization_barrier(jnp.sum(values * one_hot, axis=1))
    weight = jnp.power(jnp.float32(0.97), step_index.astype(jnp.float32)) * trace_code.astype(jnp.float32) / LEVELS
    differ = value - targets
    coef = weight * differ
    loss = 0.5 * jnp.sum(weight * differ * differ) / TOKENS
    picked = one_hot * coef[:, None]
    grad_head = jnp.dot(output.T, picked, precision=lax.Precision.HIGHEST)
    out_grad = jnp.dot(picked, critic_head.T, precision=lax.Precision.HIGHEST).astype(jnp.bfloat16)
    grad_down = jnp.dot(hidden.T, out_grad, preferred_element_type=jnp.float32)
    hidden_grad = jnp.dot(out_grad, w_down.T, preferred_element_type=jnp.float32)
    sigmoid_gate = jax.nn.sigmoid(gate)
    gate_grad = (hidden_grad * up_proj * sigmoid_gate * (1.0 + gate * (1.0 - sigmoid_gate))).astype(jnp.bfloat16)
    up_grad = (hidden_grad * jax.nn.silu(gate)).astype(jnp.bfloat16)
    grad_gate = jnp.dot(normed.T, gate_grad, preferred_element_type=jnp.float32)
    grad_up = jnp.dot(normed.T, up_grad, preferred_element_type=jnp.float32)
    return (grad_gate, grad_up, grad_down, grad_head, loss)
```

```python
import functools

import jax
import jax.numpy as jnp
from jax import lax
from jax.experimental import pallas as pl
from jax.experimental.pallas import tpu as pltpu
from jax.sharding import PartitionSpec as P

MESH = pl.DeviceIdType.MESH
F32 = jnp.float32
BF16 = jnp.bfloat16
LEVELS = 8
ROWS = 32
NT = (((1,), (1,)), ((), ()))
NN = (((1,), (0,)), ((), ()))


def dot(a, b, dims=NN):
    return lax.dot_general(a, b, dims, preferred_element_type=F32)


def two(a):
    high = a.astype(BF16)
    return high, (a - high.astype(F32)).astype(BF16)


def exchange_kernel(
    nx,
    ny,
    nz,
    resid_ref,
    attn_ref,
    gain_ref,
    w_gate_hbm,
    w_up_hbm,
    w_down_hbm,
    w_head_ref,
    info_ref,
    xct_hbm,
    q_hbm,
    h_ref,
    head_ref,
    loss_ref,
    wheadt_ref,
    w_gate,
    w_up,
    w_down,
    wt,
    x_all,
    xt,
    zsum,
    meta,
    gpart,
    grecv,
    gfull,
    hpart,
    hrecv,
    hfull,
    psum,
    rs_send,
    rs_recv,
    q_all,
    vsum,
    zcoef,
    hd_core,
    hd_x,
    hd_y,
    send_sem,
    recv_sem,
    local_sem,
):
    i = lax.axis_index("dp")
    z = lax.axis_index("ffn")
    core = i % 2
    y = (i // 2) % ny
    x = i // (2 * ny)
    own, depth = resid_ref.shape
    hidden = w_down.shape[0]
    fp = wt.shape[1]
    half = nz // 2
    tokens = own * nx * ny * 2
    chunk = tokens // nz
    rep = chunk // own
    acts = w_head_ref.shape[1]

    def at_x(k):
        return (((x + k) % nx * ny + y) * 2 + core, z)

    def at_y(k):
        return ((x * ny + (y + k) % ny) * 2 + core, z)

    def at_z(k):
        return (i, (z + k) % nz)

    sibling = ((x * ny + y) * 2 + 1 - core, z)

    next_sem = [0]
    sends = []

    def copy_pair(src, dst, landing, device):
        n = next_sem[0]
        next_sem[0] += 1
        out = pltpu.make_async_remote_copy(
            src_ref=src,
            dst_ref=dst,
            send_sem=send_sem.at[n],
            recv_sem=recv_sem.at[n],
            device_id=device,
            device_id_type=MESH,
        )
        into = pltpu.make_async_remote_copy(
            src_ref=landing,
            dst_ref=landing,
            send_sem=send_sem.at[n],
            recv_sem=recv_sem.at[n],
            device_id=device,
            device_id_type=MESH,
        )
        sends.append(out)
        return out, into

    def spread(slots, me, n, at):
        arrivals = []
        for k in range(1, n):
            out, into = copy_pair(slots.at[me], slots.at[me], slots.at[(me + n - k) % n], at(k))
            out.start()
            arrivals.append(into)
        return arrivals

    def land(arrivals):
        for into in arrivals:
            into.wait_recv()

    at_core = lambda k: sibling

    def total(slots, n):
        result = slots[0]
        for k in range(1, n):
            result = result + slots[k]
        return result

    peers = [at_x(k) for k in range(1, nx)] + [at_y(k) for k in range(1, ny)]
    peers += [at_z(k) for k in range(1, nz)] + [sibling]
    barrier = pltpu.get_barrier_semaphore()
    for peer in peers:
        pl.semaphore_signal(barrier, inc=1, device_id=peer, device_id_type=MESH)

    loads = []
    for n, (src, dst) in enumerate(((w_gate_hbm, w_gate), (w_up_hbm, w_up), (w_down_hbm, w_down))):
        load = pltpu.make_async_copy(src, dst, local_sem.at[n])
        load.start()
        loads.append(load)

    row = lax.broadcasted_iota(jnp.int32, (own, chunk), 0)
    lane = lax.broadcasted_iota(jnp.int32, (own, chunk), 1)
    row8 = lax.broadcasted_iota(jnp.int32, (8, chunk), 0)
    lane8 = lax.broadcasted_iota(jnp.int32, (8, chunk), 1)
    action_row = lax.broadcasted_iota(jnp.int32, (ROWS, chunk), 0).astype(F32)

    def lanes_of(column):
        return jnp.sum(jnp.where(lane % own == row, column, 0.0), axis=0, keepdims=True)

    def rows_of(vector):
        return jnp.sum(jnp.where(lane == row, vector, 0.0), axis=1, keepdims=True)

    def stack(*vectors):
        block = jnp.zeros((8, chunk), F32)
        for n, vector in enumerate(vectors):
            block = jnp.where(row8 == n, vector, block)
        return block

    summed = resid_ref[...].astype(F32) + attn_ref[...].astype(F32)
    squares = jnp.sum(summed * summed, axis=1, keepdims=True)
    w_head = w_head_ref[...]
    action_own = info_ref[:, 2:3]
    one_hot_own = lax.broadcasted_iota(jnp.int32, (own, acts), 1).astype(F32) == action_own
    scores = dot(resid_ref[...], w_head) + dot(attn_ref[...], w_head)
    score = jnp.sum(jnp.where(one_hot_own, scores, 0.0), axis=1, keepdims=True)
    zsum[z] = stack(lanes_of(squares), lanes_of(score))

    pl.semaphore_wait(barrier, len(peers))
    zsum_in = spread(zsum, z, nz, at_z)

    eye = (
        lax.broadcasted_iota(jnp.int32, (fp, hidden), 0)
        == lax.broadcasted_iota(jnp.int32, (fp, hidden), 1)
    ).astype(BF16)
    loads[0].wait()
    wt[0] = dot(eye, w_gate[...], NT).astype(BF16)
    loads[1].wait()
    wt[1] = dot(eye, w_up[...], NT).astype(BF16)

    land(zsum_in)
    zboth = total(zsum, nz)
    mean = rows_of(zboth[0:1]) / (depth * nz)
    normed = (summed * lax.rsqrt(mean + 1e-06) * gain_ref[...]).astype(BF16)
    hr = own // 2
    x_all[x, y, core, 0] = normed[:hr]
    x_all[x, y, core, 1] = normed[hr:]

    first_a, first_b = [], []
    for k in range(1, nx):
        mine = x_all.at[x, y, core, 0]
        out, into = copy_pair(mine, mine, x_all.at[(x + nx - k) % nx, y, core, 0], at_x(k))
        out.start()
        first_a.append(into)
    for k in range(1, ny):
        mine = x_all.at[x, y, core, 1]
        out, into = copy_pair(mine, mine, x_all.at[x, (y + ny - k) % ny, core, 1], at_y(k))
        out.start()
        first_b.append(into)

    base = lanes_of(info_ref[:, 0:1])
    mine8 = (lane8 // own == i % rep) & (jnp.full((8, chunk), i // rep, jnp.int32) == z)
    block = stack(
        zboth[1:2] - lanes_of(info_ref[:, 1:2]), base, lanes_of(action_own)
    )
    meta[0, core] = jnp.where(mine8, block, 0.0)
    meta_in = spread(meta.at[0], core, 2, at_core)

    eye_acts = (
        lax.broadcasted_iota(jnp.int32, (ROWS, acts), 0)
        == lax.broadcasted_iota(jnp.int32, (ROWS, acts), 1)
    ).astype(BF16)
    w_head_t = dot(eye_acts, w_head, NT).astype(BF16)
    wheadt_ref[...] = w_head_t

    cuts = nz // 4
    width = gpart.shape[2]

    def put_pieces(pieces, value):
        for p in range(nz):
            r, c = p // cuts, p % cuts
            pieces[p] = value[8 * r : 8 * r + 8, c * width : (c + 1) * width]

    def reduce_start(part, recv):
        arrivals = []
        for k in range(1, nz):
            out, into = copy_pair(
                part.at[(z + k) % nz], recv.at[z], recv.at[(z + nz - k) % nz], at_z(k)
            )
            out.start()
            arrivals.append(into)
        return arrivals

    def reduce_middle(arrivals, part, recv, full):
        recv[z] = part[z]
        land(arrivals)
        full[z] = total(recv, nz)
        return spread(full, z, nz, at_z)

    def pieces_of(full):
        rows = [
            jnp.concatenate([full[r * cuts + c] for c in range(cuts)], axis=1) for r in range(4)
        ]
        return jnp.concatenate(rows, axis=0)

    def wide(value):
        return jnp.concatenate(
            [value, jnp.zeros((ROWS, cuts * width - value.shape[1]), F32)], axis=1
        )

    loads[2].wait()
    put_pieces(gpart, wide(dot(w_head_t, w_down[...], NT)))
    g_in = reduce_start(gpart, grecv)

    land(first_a)
    second_a, second_b, third = [], [], []

    def pass_a(k):
        other = (y + ny - k) % ny
        part = x_all.at[:, other, core, 0]
        out, into = copy_pair(part, part, x_all.at[:, other, 1 - core, 0], sibling)
        out.start()
        third.append(into)

    def pass_b(k):
        other = (x + nx - k) % nx
        part = x_all.at[other, :, core, 1]
        out, into = copy_pair(part, part, x_all.at[other, :, 1 - core, 1], sibling)
        out.start()
        third.append(into)

    for k in range(1, ny):
        part = x_all.at[:, y, core, 0]
        out, into = copy_pair(part, part, x_all.at[:, (y + ny - k) % ny, core, 0], at_y(k))
        out.start()
        second_a.append(into)
    land(first_b)
    for k in range(1, nx):
        part = x_all.at[x, :, core, 1]
        out, into = copy_pair(part, part, x_all.at[(x + nx - k) % nx, :, core, 1], at_x(k))
        out.start()
        second_b.append(into)
    pass_a(0)
    pass_b(0)

    land(meta_in)
    meta[1, x] = meta[0, 0] + meta[0, 1]
    meta_in = spread(meta.at[1], x, nx, at_x)
    g_in = reduce_middle(g_in, gpart, grecv, gfull)

    for k in range(1, max(nx, ny)):
        if k < ny:
            second_a[k - 1].wait_recv()
            pass_a(k)
        if k < nx:
            second_b[k - 1].wait_recv()
            pass_b(k)
    land(meta_in)
    meta[2, y] = total(meta.at[1], nx)
    meta_in = spread(meta.at[2], y, ny, at_y)
    land(third)

    chips = rep // 2

    def tokens_of(c):
        rows = x_all[c * chips // ny, pl.ds(c * chips % ny, chips)]
        return rows.reshape(chunk, depth)

    hops = {(d, h): half if d == h else half - 1 for d in (0, 1) for h in (0, 1)}
    order = ((0, 0), (1, 1), (0, 1), (1, 0))
    sign = (1, -1)

    def chunk_at(offset):
        return (z + nz + offset) % nz

    waiting = {}
    for o in range(half, 0, -1):
        chosen = [dh for dh in order if hops[dh] >= o]
        for d in (0, 1):
            block = tokens_of(chunk_at(sign[d] * o))
            for h in (0, 1):
                if (d, h) in chosen:
                    psum[d, h] = dot(wt[h], block, NT)
        for d, h in chosen:
            s = hops[d, h] - o
            value = psum[d, h]
            if s > 0:
                waiting[d, h].wait_recv()
                value = value + rs_recv[d, h, s - 1].astype(F32)
            rs_send[d, h, s] = value.astype(BF16)
            out, into = copy_pair(
                rs_send.at[d, h, s], rs_recv.at[d, h, s], rs_recv.at[d, h, s], at_z(sign[d] % nz)
            )
            out.start()
            waiting[d, h] = into

    block = tokens_of(z)
    for h in (0, 1):
        psum[0, h] = dot(wt[h], block, NT)
    land(meta_in)
    info = total(meta.at[2], ny)
    land(g_in)
    g_full = jnp.transpose(pieces_of(gfull))[:fp]
    one_hot = (action_row == info[2:3]).astype(BF16)
    g_high, g_low = two(g_full)
    picked_g = dot(g_high, one_hot) + dot(g_low, one_hot)

    def all_sum(h):
        value = psum[0, h]
        for d in (h, 1 - h):
            waiting[d, h].wait_recv()
            value = value + rs_recv[d, h, hops[d, h] - 1].astype(F32)
        return value

    gate = all_sum(0)
    up = all_sum(1)
    sg = 1.0 / (1.0 + jnp.exp(-gate))
    silu = gate * sg
    lanes = pl.ds(pl.multiple_of(z * chunk, chunk), chunk)
    q_all[0, :, lanes] = (picked_g * up * sg * (1.0 + gate * (1.0 - sg))).astype(BF16)
    q_all[1, :, lanes] = (picked_g * silu).astype(BF16)

    arriving = {}

    def pass_q(d, h, s):
        def piece(c):
            return q_all.at[h, :, pl.ds(pl.multiple_of(c * chunk, chunk), chunk)]

        if s > 0:
            arriving[d, h].wait_recv()
        mine = piece(chunk_at(-sign[d] * s))
        out, into = copy_pair(
            mine, mine, piece(chunk_at(-sign[d] * (s + 1))), at_z(sign[d] % nz)
        )
        out.start()
        arriving[d, h] = into

    for d, h in order:
        pass_q(d, h, 0)

    act = (silu * up).astype(BF16).astype(F32)
    v = jnp.sum(act * picked_g, axis=0, keepdims=True)
    vsum[0, core] = stack(v)
    land(spread(vsum.at[0], core, 2, at_core))
    vsum[1, x] = vsum[0, 0] + vsum[0, 1]
    land(spread(vsum.at[1], x, nx, at_x))
    vsum[2, y] = total(vsum.at[1], nx)
    land(spread(vsum.at[2], y, ny, at_y))
    v_all = total(vsum.at[2], ny)
    differ = info[0:1] + v_all[0:1]
    weight = info[1:2]
    coef = weight * differ
    zcoef[z] = stack(coef, info[2:3], weight * differ * differ)
    zcoef_in = spread(zcoef, z, nz, at_z)

    act_high, act_low = two(act * coef)
    put_pieces(hpart, wide(dot(one_hot, act_high, NT) + dot(one_hot, act_low, NT)))
    h_in = reduce_start(hpart, hrecv)

    for d, h in order:
        if hops[d, h] > 1:
            pass_q(d, h, 1)

    land(zcoef_in)
    h_in = reduce_middle(h_in, hpart, hrecv, hfull)

    loss_rows = total(zcoef, nz)[2:3]
    loss = 0.5 * jnp.sum(loss_rows, axis=1, keepdims=True) / tokens
    loss_ref[...] = jnp.broadcast_to(loss, (8, chunk))

    out_copies = []
    for c in range(nz):
        block = jnp.transpose(tokens_of(c)).astype(F32)
        xt[:, c * chunk : (c + 1) * chunk] = (block * zcoef[c, 0:1]).astype(BF16)
    out = pltpu.make_async_copy(xt, xct_hbm, local_sem.at[3])
    out.start()
    out_copies.append(out)

    land(h_in)
    h_sum = pieces_of(hfull)
    h_ref[...] = jnp.transpose(h_sum)

    h_high, h_low = two(h_sum[:, :hidden])
    head = dot(h_high, w_down[...]) + dot(h_low, w_down[...])
    own_block = zcoef[i // rep]
    lane32 = lax.broadcasted_iota(jnp.int32, (ROWS, chunk), 1)
    picked = jnp.where(
        (action_row == own_block[1:2]) & (lane32 // own == i % rep), own_block[0:1], 0.0
    )
    p_high, p_low = two(picked)
    for ref in (resid_ref, attn_ref):
        rows = jnp.concatenate([ref[...]] * rep, axis=0)
        head = head + dot(p_high, rows) + dot(p_low, rows)
    wide_half = depth // 2
    for c in (0, 1):
        hd_core[c] = head[: hd_core.shape[1], c * wide_half : (c + 1) * wide_half]
    out, into = copy_pair(hd_core.at[1 - core], hd_core.at[2], hd_core.at[2], sibling)
    out.start()

    for s in range(2, half):
        if s == 2:
            into.wait_recv()
            hd_x[x] = hd_core[core] + hd_core[2]
            hd_in = spread(hd_x, x, nx, at_x)
        for d, h in order:
            if hops[d, h] > s:
                pass_q(d, h, s)
        if s == 2:
            land(hd_in)
            hd_y[y] = total(hd_x, nx)
            hd_in = spread(hd_y, y, ny, at_y)
    if half <= 2:
        into.wait_recv()
        hd_x[x] = hd_core[core] + hd_core[2]
        land(spread(hd_x, x, nx, at_x))
        hd_y[y] = total(hd_x, nx)
        hd_in = spread(hd_y, y, ny, at_y)
    land(hd_in)
    hd_core[3 + core] = total(hd_y, ny)
    out, into = copy_pair(
        hd_core.at[3 + core], hd_core.at[3 + core], hd_core.at[4 - core], sibling
    )
    out.start()
    into.wait_recv()
    head_ref[...] = jnp.concatenate([hd_core[3], hd_core[4]], axis=1)

    for d, h in order:
        arriving[d, h].wait_recv()
    out = pltpu.make_async_copy(q_all, q_hbm, local_sem.at[4])
    out.start()
    out_copies.append(out)
    for out in sends:
        out.wait_send()
    for out in out_copies:
        out.wait()


def grads_kernel(xct_ref, q_ref, h_ref, head_ref, loss_ref, wheadt_ref, gg, gu, gd, gh, loss):
    hidden, acts = gd.shape[0], gh.shape[1]
    fp = q_ref.shape[1]
    block = xct_ref[...]
    gg[...] = dot(block, q_ref[0], NT)[:, :hidden]
    gu[...] = dot(block, q_ref[1], NT)[:, :hidden]
    h_high, h_low = two(h_ref[:fp])
    head_t = wheadt_ref[...]
    gd[...] = (dot(h_high, head_t) + dot(h_low, head_t))[:hidden]
    gh[...] = jnp.transpose(head_ref[...])[:, :acts]
    loss[0, 0] = loss_ref[0, 0]


def body(
    nx,
    ny,
    nz,
    resid,
    attn_out,
    norm_gain,
    w_gate,
    w_up,
    w_down,
    w_head,
    actions,
    step_index,
    trace_code,
    targets,
):
    own, depth = resid.shape
    hidden = w_down.shape[0]
    acts = w_head.shape[1]
    fp = -(-hidden // 16) * 16
    fl = -(-hidden // 128) * 128
    tokens = own * nx * ny * 2
    chunk = tokens // nz
    half = nz // 2
    cuts = nz // 4
    head_rows = -(-acts // 8) * 8
    weight = (
        jnp.power(jnp.float32(0.97), step_index.astype(F32)) * trace_code.astype(F32) / LEVELS
    )
    info = jnp.stack([weight, targets, actions.astype(F32)], axis=1)
    info = jnp.pad(info, ((0, 0), (0, 125)))
    vmem = pl.BlockSpec(memory_space=pltpu.VMEM)
    anywhere = pl.BlockSpec(memory_space=pl.ANY)
    shape = jax.ShapeDtypeStruct
    n_sems = (
        2 * (nx - 1 + ny - 1) + nx + ny + 3 * (1 + nx - 1 + ny - 1) + 1 + 6 * (nz - 1)
        + 2 * 2 * (2 * half - 1)
    )
    pieces = pltpu.VMEM((nz, 8, fl // cuts), F32)
    xct, q, h, head, loss, w_head_t = pl.pallas_call(
        functools.partial(exchange_kernel, nx, ny, nz),
        out_shape=(
            shape((depth, tokens), BF16),
            shape((2, fp, tokens), BF16),
            shape((fl, ROWS), F32),
            shape((head_rows, depth), F32),
            shape((8, chunk), F32),
            shape((ROWS, depth), BF16),
        ),
        in_specs=[vmem, vmem, vmem, anywhere, anywhere, anywhere, vmem, vmem],
        out_specs=(anywhere, anywhere, vmem, vmem, vmem, vmem),
        scratch_shapes=[
            pltpu.VMEM(w_gate.shape, BF16),
            pltpu.VMEM(w_up.shape, BF16),
            pltpu.VMEM(w_down.shape, BF16),
            pltpu.VMEM((2, fp, depth), BF16),
            pltpu.VMEM((nx, ny, 2, 2, own // 2, depth), BF16),
            pltpu.VMEM((depth, tokens), BF16),
            pltpu.VMEM((nz, 8, chunk), F32),
            pltpu.VMEM((3, max(nx, ny), 8, chunk), F32),
            pieces,
            pieces,
            pieces,
            pieces,
            pieces,
            pieces,
            pltpu.VMEM((2, 2, fp, chunk), F32),
            pltpu.VMEM((2, 2, half, fp, chunk), BF16),
            pltpu.VMEM((2, 2, half, fp, chunk), BF16),
            pltpu.VMEM((2, fp, tokens), BF16),
            pltpu.VMEM((3, max(nx, ny), 8, chunk), F32),
            pltpu.VMEM((nz, 8, chunk), F32),
            pltpu.VMEM((5, head_rows, depth // 2), F32),
            pltpu.VMEM((nx, head_rows, depth // 2), F32),
            pltpu.VMEM((ny, head_rows, depth // 2), F32),
            pltpu.SemaphoreType.DMA((n_sems,)),
            pltpu.SemaphoreType.DMA((n_sems,)),
            pltpu.SemaphoreType.DMA((5,)),
        ],
        compiler_params=pltpu.CompilerParams(
            collective_id=0, has_side_effects=True, vmem_limit_bytes=40 * 1024 * 1024
        ),
        name="exchange",
    )(resid, attn_out, norm_gain.reshape(1, depth), w_gate, w_up, w_down, w_head, info)

    tile = min(256, depth)
    grad_gate, grad_up, grad_down, grad_head, loss = pl.pallas_call(
        grads_kernel,
        grid=(depth // tile,),
        out_shape=(
            shape((depth, hidden), F32),
            shape((depth, hidden), F32),
            shape((hidden, depth), F32),
            shape((depth, acts), F32),
            shape((1, 1), F32),
        ),
        in_specs=[
            pl.BlockSpec((tile, tokens), lambda n: (n, 0)),
            pl.BlockSpec((2, fp, tokens), lambda n: (0, 0, 0)),
            pl.BlockSpec((fl, ROWS), lambda n: (0, 0)),
            pl.BlockSpec((head_rows, tile), lambda n: (0, n)),
            pl.BlockSpec((8, chunk), lambda n: (0, 0)),
            pl.BlockSpec((ROWS, tile), lambda n: (0, n)),
        ],
        out_specs=(
            pl.BlockSpec((tile, hidden), lambda n: (n, 0)),
            pl.BlockSpec((tile, hidden), lambda n: (n, 0)),
            pl.BlockSpec((hidden, tile), lambda n: (0, n)),
            pl.BlockSpec((tile, acts), lambda n: (n, 0)),
            pl.BlockSpec((1, 1), lambda n: (0, 0), memory_space=pltpu.SMEM),
        ),
        compiler_params=pltpu.CompilerParams(vmem_limit_bytes=40 * 1024 * 1024),
        name="weight_grads",
    )(xct, q, h, head, loss, w_head_t)
    return grad_gate, grad_up, grad_down, grad_head, loss.reshape(())


def build(mesh, nx, ny):
    nz = mesh.shape["ffn"]
    in_specs = (
        P("dp", "ffn"),
        P("dp", "ffn"),
        P("ffn"),
        P("ffn", "dp"),
        P("ffn", "dp"),
        P("dp", "ffn"),
        P("ffn", None),
        P("dp"),
        P("dp"),
        P("dp"),
        P("dp"),
    )
    out_specs = (P("ffn", "dp"), P("ffn", "dp"), P("dp", "ffn"), P("ffn", None), P())
    return jax.shard_map(
        functools.partial(body, nx, ny, nz),
        mesh=mesh,
        in_specs=in_specs,
        out_specs=out_specs,
        check_vma=False,
    )


def solution(mesh):
    return build(mesh, 4, 4)
```

```python
import functools

import jax
import jax.numpy as jnp
from jax import lax
from jax.experimental import pallas as pl
from jax.experimental.pallas import tpu as pltpu
from jax.sharding import PartitionSpec as P

MESH = pl.DeviceIdType.MESH
F32 = jnp.float32
BF16 = jnp.bfloat16
LEVELS = 8
ROWS = 32
NT = (((1,), (1,)), ((), ()))
NN = (((1,), (0,)), ((), ()))


def dot(a, b, dims=NN):
    return lax.dot_general(a, b, dims, preferred_element_type=F32)


def two(a):
    high = a.astype(BF16)
    return high, (a - high.astype(F32)).astype(BF16)


def exchange_kernel(
    nx,
    ny,
    nz,
    *refs,
):
    sources, refs = refs[:11], refs[11:]
    body_of_exchange(nx, ny, nz, sources, *refs)


def body_of_exchange(
    nx,
    ny,
    nz,
    sources,
    x_out,
    q_out,
    h_ref,
    head_ref,
    loss_ref,
    wheadt_ref,
    resid_ref,
    attn_ref,
    gain_ref,
    w_both,
    w_down,
    w_head_ref,
    actions_ref,
    step_ref,
    trace_ref,
    targets_ref,
    xs,
    x_mat,
    sel,
    zsum,
    meta,
    meta2,
    gpart,
    grecv,
    gfull,
    hpart,
    psum,
    rs_send,
    rs_recv,
    q_all,
    q_scaled,
    vsum,
    vsum2,
    zcoef,
    hd_part,
    hd_recv,
    hd_y,
    hd_full,
    send_sem,
    recv_sem,
    local_sem,
):
    i = lax.axis_index("dp")
    z = lax.axis_index("ffn")
    core = i % 2
    y = (i // 2) % ny
    x = i // (2 * ny)
    own, depth = resid_ref.shape
    hidden = w_down.shape[0]
    fp = q_all.shape[1]
    half = nz // 2
    tokens = own * nx * ny * 2
    chunk = tokens // nz
    share = own // nz
    bands = 16 // share
    band = depth // bands
    acts = w_head_ref.shape[0]

    def at_x(k):
        return (((x + k) % nx * ny + y) * 2 + core, z)

    def at_y(k):
        return ((x * ny + (y + k) % ny) * 2 + core, z)

    def at_xy(kx, ky):
        return (((x + kx) % nx * ny + (y + ky) % ny) * 2 + core, z)

    def at_z(k):
        return (i, (z + k) % nz)

    sibling = ((x * ny + y) * 2 + 1 - core, z)

    next_sem = [0]
    sends = []

    def copy_pair(src, dst, landing, device):
        n = next_sem[0]
        next_sem[0] += 1
        out = pltpu.make_async_remote_copy(
            src_ref=src,
            dst_ref=dst,
            send_sem=send_sem.at[n],
            recv_sem=recv_sem.at[n],
            device_id=device,
            device_id_type=MESH,
        )
        into = pltpu.make_async_remote_copy(
            src_ref=landing,
            dst_ref=landing,
            send_sem=send_sem.at[n],
            recv_sem=recv_sem.at[n],
            device_id=device,
            device_id_type=MESH,
        )
        sends.append(out)
        return out, into

    def spread(slots, me, n, at):
        arrivals = []
        for k in range(1, n):
            out, into = copy_pair(slots.at[me], slots.at[me], slots.at[(me + n - k) % n], at(k))
            out.start()
            arrivals.append(into)
        return arrivals

    def land(arrivals):
        for into in arrivals:
            into.wait_recv()

    group = 2 * x + core

    def mates():
        for k in range(nx):
            for flip in (0, 1):
                if k or flip:
                    other = core + flip - 2 * core * flip
                    device = (((x + k) % nx * ny + y) * 2 + other, z)
                    yield device, (x + k) % nx * 2 + other, (x + nx - k) % nx * 2 + other

    def spread_row(slots):
        arrivals = []
        for device, _, source in mates():
            out, into = copy_pair(slots.at[group], slots.at[group], slots.at[source], device)
            out.start()
            arrivals.append(into)
        return arrivals

    def total(slots, n):
        result = slots[0]
        for k in range(1, n):
            result = result + slots[k]
        return result

    peers = [device for device, _, _ in mates()] + [at_z(k) for k in range(1, nz)]
    peers += [at_xy(kx, ky) for kx in range(nx) for ky in range(1, ny)]
    barrier = pltpu.get_barrier_semaphore()
    for peer in peers:
        pl.semaphore_signal(barrier, inc=1, device_id=peer, device_id_type=MESH)

    places = (
        resid_ref,
        attn_ref,
        gain_ref,
        w_both.at[0],
        w_both.at[1],
        w_down,
        w_head_ref,
        actions_ref,
        step_ref,
        trace_ref,
        targets_ref,
    )
    loads = [
        pltpu.make_async_copy(src, dst, local_sem.at[n])
        for n, (src, dst) in enumerate(zip(sources, places))
    ]
    for n in (0, 1, 6, 7, 8, 9, 10, 2, 3, 4, 5):
        loads[n].start()

    row = lax.broadcasted_iota(jnp.int32, (own, chunk), 0)
    lane = lax.broadcasted_iota(jnp.int32, (own, chunk), 1)
    row8 = lax.broadcasted_iota(jnp.int32, (8, chunk), 0)
    action_row = lax.broadcasted_iota(jnp.int32, (ROWS, chunk), 0).astype(F32)

    def lanes_of(column):
        return jnp.sum(jnp.where(lane % own == row, column, 0.0), axis=0, keepdims=True)

    def rows_of(vector):
        return jnp.sum(jnp.where(lane == row, vector, 0.0), axis=1, keepdims=True)

    def column_of(vector):
        same = lane[:, :own] == row[:, :own]
        return jnp.sum(jnp.where(same, vector, 0.0), axis=1, keepdims=True)

    def stack(*vectors):
        block = jnp.zeros((8, chunk), F32)
        for n, vector in enumerate(vectors):
            block = jnp.where(row8 == n, vector, block)
        return block

    for n in (0, 1, 6, 7, 8, 9, 10, 2):
        loads[n].wait()
    cuts = nz // 4
    width = gpart.shape[2]

    def put_pieces(pieces, value):
        for p in range(nz):
            r, c = p // cuts, p % cuts
            pieces[p] = value[8 * r : 8 * r + 8, c * width : (c + 1) * width]

    def reduce_start(part, recv):
        arrivals = []
        for k in range(1, nz):
            out, into = copy_pair(
                part.at[(z + k) % nz], recv.at[z], recv.at[(z + nz - k) % nz], at_z(k)
            )
            out.start()
            arrivals.append(into)
        return arrivals

    def reduce_middle(arrivals, part, recv, full):
        recv[z] = part[z]
        land(arrivals)
        full[z] = total(recv, nz)
        return spread(full, z, nz, at_z)

    def pieces_of(full):
        rows = [
            jnp.concatenate([full[r * cuts + c] for c in range(cuts)], axis=1) for r in range(4)
        ]
        return jnp.concatenate(rows, axis=0)

    def wide(value):
        return jnp.concatenate(
            [value, jnp.zeros((ROWS, cuts * width - value.shape[1]), F32)], axis=1
        )

    summed = resid_ref[...].astype(F32) + attn_ref[...].astype(F32)
    squares = jnp.sum(summed * summed, axis=1, keepdims=True)
    eye_acts = (
        lax.broadcasted_iota(jnp.int32, (ROWS, acts), 0)
        == lax.broadcasted_iota(jnp.int32, (ROWS, acts), 1)
    ).astype(BF16)
    w_head_t = dot(eye_acts, w_head_ref[...]).astype(BF16)
    action_own = column_of(actions_ref[...].astype(F32))
    weight_own = column_of(
        jnp.power(jnp.float32(0.97), step_ref[...].astype(F32)) * trace_ref[...].astype(F32) / LEVELS
    )
    target_own = column_of(targets_ref[...])
    one_hot_own = lax.broadcasted_iota(jnp.int32, (own, ROWS), 1).astype(F32) == action_own
    scores = dot(resid_ref[...], w_head_t, NT) + dot(attn_ref[...], w_head_t, NT)
    score = jnp.sum(jnp.where(one_hot_own, scores, 0.0), axis=1, keepdims=True)
    zsum[z] = stack(lanes_of(squares), lanes_of(score))

    pl.semaphore_wait(barrier, len(peers))
    zsum_in = spread(zsum, z, nz, at_z)

    loads[5].wait()
    put_pieces(gpart, wide(dot(w_head_t, w_down[...], NT)))
    g_in = reduce_start(gpart, grecv)
    psum[...] = jnp.zeros_like(psum)
    to = lax.broadcasted_iota(jnp.int32, (chunk, 16 * chunk // share), 0)
    come = lax.broadcasted_iota(jnp.int32, (chunk, 16 * chunk // share), 1)
    for g in range(bands):
        sel[g] = (come == to // share * 16 + g * share + to % share).astype(BF16)
    wheadt_ref[...] = w_head_t

    land(zsum_in)
    zboth = total(zsum, nz)
    mean = rows_of(zboth[0:1]) / (depth * nz)
    normed = (summed * lax.rsqrt(mean + 1e-06) * gain_ref[...]).astype(BF16)

    count = nz * 16
    line = lax.broadcasted_iota(jnp.int32, (count, own), 0)
    place = line // 16
    even = half - place // 2
    offset = jnp.where(place % 2 == 0, -even, half - (place + 1) // 2)
    token = (z + offset + nz) % nz * share + line % share
    token_at = lax.broadcasted_iota(jnp.int32, (count, own), 1) == token
    packed = jnp.zeros((count, band), F32)
    for g in range(bands):
        pick = (token_at & (line % 16 // share == g)).astype(BF16)
        packed = packed + dot(pick, normed[:, g * band : (g + 1) * band])
    chip = x * ny + y
    xs[chip, core] = packed.astype(BF16).reshape(nz, 16, band)

    groups = ((0, 1), (1, 1 + half), (1 + half, nz))
    near_first = lambda n: sorted(range(n), key=lambda k: min(k, n - k))
    coming, third = {}, {}

    def send_group(n):
        places = pl.ds(groups[n][0], groups[n][1] - groups[n][0])
        coming[n] = []
        mine = xs.at[chip, core, places]
        for kx in near_first(nx):
            for ky in near_first(ny):
                if kx or ky:
                    source = (x + nx - kx) % nx * ny + (y + ny - ky) % ny
                    out, into = copy_pair(mine, mine, xs.at[source, core, places], at_xy(kx, ky))
                    out.start()
                    coming[n].append(into)

    def pass_group(n):
        places = pl.ds(groups[n][0], groups[n][1] - groups[n][0])
        land(coming[n])
        mine = xs.at[:, core, places]
        out, third[n] = copy_pair(mine, mine, xs.at[:, 1 - core, places], sibling)
        out.start()

    def gather(r):
        rows = xs[:, :, r].reshape(16 * chunk // share, band)
        for g in range(bands):
            x_mat[r, :, g * band : (g + 1) * band] = dot(sel[g], rows).astype(BF16)

    send_group(0)
    send_group(1)

    here = (row == share * z + lane % share) & (lane // share == i)

    def chunk_of(column):
        return jnp.sum(jnp.where(here, column, 0.0), axis=0, keepdims=True)

    base = rows_of(zboth[1:2]) - target_own
    meta[group] = stack(chunk_of(base), chunk_of(weight_own), chunk_of(action_own))
    meta_in = spread_row(meta)

    pass_group(0)
    send_group(2)
    third[0].wait_recv()

    hops = {(d, h): half if d == h else half - 1 for d in (0, 1) for h in (0, 1)}
    order = ((0, 0), (1, 1), (0, 1), (1, 0))
    sign = (1, -1)

    def chunk_at(offset):
        return (z + nz + offset) % nz

    loads[3].wait()
    loads[4].wait()
    waiting = {}
    cut = -(-fp // 32) * 16
    parts = (slice(0, cut), slice(cut, fp))
    for o in range(half, 0, -1):
        chosen = [dh for dh in order if hops[dh] >= o]
        if o == half - 1:
            third[1].wait_recv()
        if o == half // 2 - 1:
            third[2].wait_recv()
        if o < half:
            gather(2 * (half - o) - 1)
        gather(2 * (half - o))
        for d in (0, 1):
            r = 2 * (half - o) - 1 if d == 0 and o < half else 2 * (half - o)
            for h in (0, 1):
                if (d, h) in chosen:
                    psum[d, h, :hidden] = dot(w_both[h], x_mat[r], NT)
        for p, rows in enumerate(parts):
            for d, h in chosen:
                s = hops[d, h] - o
                value = psum[d, h, rows]
                if s > 0:
                    waiting[d, h, p].wait_recv()
                    value = value + rs_recv[d, h, s - 1, rows].astype(F32)
                rs_send[d, h, s, rows] = value.astype(BF16)
                landing = rs_recv.at[d, h, s, rows]
                out, into = copy_pair(
                    rs_send.at[d, h, s, rows], landing, landing, at_z(sign[d] % nz)
                )
                out.start()
                waiting[d, h, p] = into

        if o == half:
            land(meta_in)
            meta2[y] = total(meta, 2 * nx)
            meta_in = spread(meta2, y, ny, at_y)
            g_in = reduce_middle(g_in, gpart, grecv, gfull)
            pass_group(1)
        if o == half - 1:
            pass_group(2)

    if half < 4:
        third[2].wait_recv()
    gather(nz - 1)
    for h in (0, 1):
        psum[0, h, :hidden] = dot(w_both[h], x_mat[nz - 1], NT)
    land(meta_in)
    info = total(meta2, ny)
    land(g_in)
    g_full = jnp.transpose(pieces_of(gfull))[:fp]
    one_hot = (action_row == info[2:3]).astype(BF16)
    g_high, g_low = two(g_full)
    picked_g = dot(g_high, one_hot) + dot(g_low, one_hot)

    lanes = pl.ds(pl.multiple_of(z * chunk, chunk), chunk)
    arriving = {}

    def pass_q(d, h, s, p):
        def piece(c):
            return q_all.at[h, parts[p], pl.ds(pl.multiple_of(c * chunk, chunk), chunk)]

        if s > 0:
            arriving[d, h, p].wait_recv()
        mine = piece(chunk_at(-sign[d] * s))
        out, into = copy_pair(
            mine, mine, piece(chunk_at(-sign[d] * (s + 1))), at_z(sign[d] % nz)
        )
        out.start()
        arriving[d, h, p] = into

    def pass_on(s, p):
        for d, h in order:
            if hops[d, h] > s:
                pass_q(d, h, s, p)

    acts_of = []
    v = jnp.zeros((1, chunk), F32)
    for p, rows in enumerate(parts):
        sums = []
        for h in (0, 1):
            value = psum[0, h, rows]
            for d in (h, 1 - h):
                waiting[d, h, p].wait_recv()
                value = value + rs_recv[d, h, hops[d, h] - 1, rows].astype(F32)
            sums.append(value)
        gate, up = sums
        sg = 1.0 / (1.0 + jnp.exp(-gate))
        silu = gate * sg
        part_g = picked_g[rows]
        q_all[0, rows, lanes] = (part_g * up * sg * (1.0 + gate * (1.0 - sg))).astype(BF16)
        q_all[1, rows, lanes] = (part_g * silu).astype(BF16)
        act = (silu * up).astype(BF16).astype(F32)
        acts_of.append(act)
        v = v + jnp.sum(act * part_g, axis=0, keepdims=True)
        if p == 0:
            pass_on(0, 0)

    vsum[group] = stack(v)
    v_in = spread_row(vsum)
    pass_on(0, 1)
    act = jnp.concatenate(acts_of, axis=0)
    out_copies = []
    for r in range(nz):
        c = chunk_at(-(half - r // 2) if r % 2 == 0 else half - (r + 1) // 2)
        out = pltpu.make_async_copy(x_mat.at[r], x_out.at[c], local_sem.at[11 + r])
        out.start()
        out_copies.append(out)
    pass_on(1, 0)
    land(v_in)
    vsum2[y] = total(vsum, 2 * nx)
    v_in = spread(vsum2, y, ny, at_y)
    pass_on(1, 1)
    land(v_in)
    v_all = total(vsum2, ny)
    differ = info[0:1] + v_all[0:1]
    weight = info[1:2]
    coef = weight * differ

    fl = cuts * width
    strips = fl // 128
    row16 = lax.broadcasted_iota(jnp.int32, (16, 128), 0)
    row16_wide = lax.broadcasted_iota(jnp.int32, (16, fl), 0)

    def put_h(value):
        hpart[z, :, :fl] = value[:16].astype(BF16)
        beside = jnp.zeros((16, 128), F32)
        for n in range((acts - 16) * strips):
            a, k = 16 + n // strips, n % strips
            strip = value[a : a + 1, 128 * k : 128 * k + 128]
            beside = jnp.where(row16 == n, strip, beside)
        hpart[z, :, fl:] = beside.astype(BF16)

    def sum_h():
        value = hpart[0].astype(F32)
        for k in range(1, nz):
            value = value + hpart[k].astype(F32)
        last = jnp.zeros((16, fl), F32)
        for a in range(acts - 16):
            strip = [value[a * strips + k : a * strips + k + 1, fl:] for k in range(strips)]
            last = jnp.where(row16_wide == a, jnp.concatenate(strip, axis=1), last)
        return jnp.concatenate([value[:, :fl], last], axis=0)

    act_high, act_low = two(act * coef)
    put_h(wide(dot(one_hot, act_high, NT) + dot(one_hot, act_low, NT)))
    h_in = spread(hpart, z, nz, at_z)
    zcoef[z] = stack(coef, info[2:3], weight * differ * differ)
    zcoef_in = spread(zcoef, z, nz, at_z)
    for p in (0, 1):
        if half > 2:
            pass_on(2, p)

    land(zcoef_in)
    coef_own = jnp.zeros((own, chunk), F32)
    for c in range(nz):
        mine = (row // share == c) & (lane == i * share + row % share)
        coef_own = jnp.where(mine, zcoef[c, 0:1], coef_own)
    coef_own = jnp.sum(coef_own, axis=1, keepdims=True)
    coef_lanes = jnp.sum(
        jnp.where(lane[:, :own] == row[:, :own], coef_own, 0.0), axis=0, keepdims=True
    )
    picked = jnp.where(
        action_row[:, :own] == actions_ref[...].astype(F32), coef_lanes, 0.0
    )
    p_high, p_low = two(picked)
    head = jnp.zeros((ROWS, depth), F32)
    for ref in (resid_ref, attn_ref):
        head = head + dot(p_high, ref[...]) + dot(p_low, ref[...])
    for s in range(3, half):
        pass_on(s, 0)
        pass_on(s, 1)
    land(h_in)
    h_sum = sum_h()
    h_high, h_low = two(h_sum[:, :hidden])
    head = head + dot(h_high, w_down[...]) + dot(h_low, w_down[...])
    head_rows, piece = hd_part.shape[1:]
    for g in range(2 * nx):
        hd_part[g] = head[:head_rows, g * piece : (g + 1) * piece]
    hd_recv[group] = hd_part[group]
    hd_in = []
    for device, target, source in mates():
        out, into = copy_pair(hd_part.at[target], hd_recv.at[group], hd_recv.at[source], device)
        out.start()
        hd_in.append(into)

    def scale(c, n):
        lanes = pl.ds(pl.multiple_of(c * chunk, chunk), chunk)
        q_scaled[:, :, lanes] = (q_all[:, :, lanes].astype(F32) * zcoef[c, 0:1]).astype(BF16)
        out = pltpu.make_async_copy(
            q_scaled.at[:, :, lanes], q_out.at[:, :, lanes], local_sem.at[11 + nz + n]
        )
        out.start()
        out_copies.append(out)

    scale(z, 0)
    n = 1
    for o in range(1, half - 1):
        scale(chunk_at(o), n)
        scale(chunk_at(-o), n + 1)
        n += 2
    h_ref[...] = jnp.transpose(h_sum)
    loss = 0.5 * jnp.sum(total(zcoef, nz)[2:3], axis=1, keepdims=True) / tokens
    loss_ref[...] = jnp.broadcast_to(loss, (8, chunk))
    land(hd_in)
    hd_y[y] = total(hd_recv, 2 * nx)
    hd_in = spread(hd_y, y, ny, at_y)
    for d, h in order[2:]:
        for p in (0, 1):
            arriving[d, h, p].wait_recv()
    scale(chunk_at(half - 1), n)
    scale(chunk_at(1 - half), n + 1)
    for d, h in order[:2]:
        for p in (0, 1):
            arriving[d, h, p].wait_recv()
    scale(chunk_at(half), n + 2)
    land(hd_in)
    hd_full[group] = total(hd_y, ny)
    land(spread_row(hd_full))
    head_ref[...] = jnp.concatenate([hd_full[g] for g in range(2 * nx)], axis=1)
    for out in sends:
        out.wait_send()
    for out in out_copies:
        out.wait()


def grads_kernel(x_ref, q_ref, h_ref, head_ref, loss_ref, wheadt_ref, gg, gu, gd, gh, loss):
    hidden, acts = gd.shape[0], gh.shape[0]
    fp = q_ref.shape[1]
    block = x_ref[...]
    gg[...] = dot(q_ref[0], block)[:hidden]
    gu[...] = dot(q_ref[1], block)[:hidden]
    h_high, h_low = two(h_ref[:fp])
    head_t = wheadt_ref[...]
    gd[...] = (dot(h_high, head_t) + dot(h_low, head_t))[:hidden]
    gh[...] = head_ref[:acts]
    loss[0, 0] = loss_ref[0, 0]


def body(
    nx,
    ny,
    nz,
    resid,
    attn_out,
    norm_gain,
    w_gate,
    w_up,
    w_down,
    w_head,
    actions,
    step_index,
    trace_code,
    targets,
):
    own, depth = resid.shape
    hidden = w_down.shape[0]
    acts = w_head.shape[1]
    fp = -(-hidden // 16) * 16
    fl = -(-hidden // 128) * 128
    tokens = own * nx * ny * 2
    chunk = tokens // nz
    share = own // nz
    bands = 16 // share
    half = nz // 2
    cuts = nz // 4
    head_rows = -(-acts // 8) * 8
    vmem = pl.BlockSpec(memory_space=pltpu.VMEM)
    anywhere = pl.BlockSpec(memory_space=pl.ANY)
    shape = jax.ShapeDtypeStruct
    n_sems = (
        3 * nx * ny + 4 * (2 * nx - 1) + 3 * (ny - 1)
        + 5 * (nz - 1)
        + 4 * 2 * (2 * half - 1)
    )
    pieces = pltpu.VMEM((nz, 8, fl // cuts), F32)
    row_slots = pltpu.VMEM((2 * nx, 8, chunk), F32)
    y_slots = pltpu.VMEM((ny, 8, chunk), F32)
    head_row = pltpu.VMEM((2 * nx, head_rows, depth // (2 * nx)), F32)
    x_out, q, h, head, loss, w_head_t = pl.pallas_call(
        functools.partial(exchange_kernel, nx, ny, nz),
        out_shape=(
            shape((nz, chunk, depth), BF16),
            shape((2, fp, tokens), BF16),
            shape((fl, ROWS), F32),
            shape((head_rows, depth), F32),
            shape((8, chunk), F32),
            shape((ROWS, depth), BF16),
        ),
        in_specs=[pl.BlockSpec(memory_space=pltpu.HBM)] * 11,
        out_specs=(anywhere, anywhere, vmem, vmem, vmem, vmem),
        scratch_shapes=[
            pltpu.VMEM((own, depth), BF16),
            pltpu.VMEM((own, depth), BF16),
            pltpu.VMEM((1, depth), F32),
            pltpu.VMEM((2, hidden, depth), BF16),
            pltpu.VMEM((hidden, depth), BF16),
            pltpu.VMEM((acts, depth), BF16),
            pltpu.VMEM((1, own), jnp.int32),
            pltpu.VMEM((1, own), jnp.int32),
            pltpu.VMEM((1, own), jnp.int32),
            pltpu.VMEM((1, own), F32),
            pltpu.VMEM((nx * ny, 2, nz, 16, depth // bands), BF16),
            pltpu.VMEM((nz, chunk, depth), BF16),
            pltpu.VMEM((bands, chunk, 16 * chunk // share), BF16),
            pltpu.VMEM((nz, 8, chunk), F32),
            row_slots,
            y_slots,
            pieces,
            pieces,
            pieces,
            pltpu.VMEM((nz, 16, fl + 128), BF16),
            pltpu.VMEM((2, 2, fp, chunk), F32),
            pltpu.VMEM((2, 2, half, fp, chunk), BF16),
            pltpu.VMEM((2, 2, half, fp, chunk), BF16),
            pltpu.VMEM((2, fp, tokens), BF16),
            pltpu.VMEM((2, fp, tokens), BF16),
            row_slots,
            y_slots,
            pltpu.VMEM((nz, 8, chunk), F32),
            head_row,
            head_row,
            pltpu.VMEM((ny, head_rows, depth // (2 * nx)), F32),
            head_row,
            pltpu.SemaphoreType.DMA((n_sems,)),
            pltpu.SemaphoreType.DMA((n_sems,)),
            pltpu.SemaphoreType.DMA((11 + 2 * nz,)),
        ],
        compiler_params=pltpu.CompilerParams(
            collective_id=0, has_side_effects=True, vmem_limit_bytes=60 * 1024 * 1024
        ),
        name="exchange",
    )(
        resid,
        attn_out,
        norm_gain.reshape(1, depth),
        w_gate.T,
        w_up.T,
        w_down,
        w_head.T,
        actions.reshape(1, own),
        step_index.reshape(1, own),
        trace_code.reshape(1, own),
        targets.reshape(1, own),
    )

    tile = min(256, depth)
    grad_gate, grad_up, grad_down, grad_head, loss = pl.pallas_call(
        grads_kernel,
        grid=(depth // tile,),
        out_shape=(
            shape((hidden, depth), F32),
            shape((hidden, depth), F32),
            shape((hidden, depth), F32),
            shape((acts, depth), F32),
            shape((1, 1), F32),
        ),
        in_specs=[
            pl.BlockSpec((tokens, tile), lambda n: (0, n)),
            pl.BlockSpec((2, fp, tokens), lambda n: (0, 0, 0)),
            pl.BlockSpec((fl, ROWS), lambda n: (0, 0)),
            pl.BlockSpec((head_rows, tile), lambda n: (0, n)),
            pl.BlockSpec((8, chunk), lambda n: (0, 0)),
            pl.BlockSpec((ROWS, tile), lambda n: (0, n)),
        ],
        out_specs=(
            pl.BlockSpec((hidden, tile), lambda n: (0, n)),
            pl.BlockSpec((hidden, tile), lambda n: (0, n)),
            pl.BlockSpec((hidden, tile), lambda n: (0, n)),
            pl.BlockSpec((acts, tile), lambda n: (0, n)),
            pl.BlockSpec((1, 1), lambda n: (0, 0), memory_space=pltpu.SMEM),
        ),
        compiler_params=pltpu.CompilerParams(vmem_limit_bytes=60 * 1024 * 1024),
        name="weight_grads",
    )(x_out.reshape(tokens, depth), q, h, head, loss, w_head_t)
    return grad_gate.T, grad_up.T, grad_down, grad_head.T, loss.reshape(())


def build(mesh, nx, ny):
    nz = mesh.shape["ffn"]
    in_specs = (
        P("dp", "ffn"),
        P("dp", "ffn"),
        P("ffn"),
        P("ffn", "dp"),
        P("ffn", "dp"),
        P("dp", "ffn"),
        P("ffn", None),
        P("dp"),
        P("dp"),
        P("dp"),
        P("dp"),
    )
    out_specs = (P("ffn", "dp"), P("ffn", "dp"), P("dp", "ffn"), P("ffn", None), P())
    return jax.shard_map(
        functools.partial(body, nx, ny, nz),
        mesh=mesh,
        in_specs=in_specs,
        out_specs=out_specs,
        check_vma=False,
    )


def solution(mesh):
    return build(mesh, 4, 4)
```

```python
import functools

import jax
import jax.numpy as jnp
from jax import lax
from jax.experimental import pallas as pl
from jax.experimental.pallas import tpu as pltpu
from jax.sharding import PartitionSpec as P

MESH = pl.DeviceIdType.MESH
F32 = jnp.float32
BF16 = jnp.bfloat16
LEVELS = 8
ROWS = 32
NT = (((1,), (1,)), ((), ()))
NN = (((1,), (0,)), ((), ()))


def dot(a, b, dims=NN):
    return lax.dot_general(a, b, dims, preferred_element_type=F32)


def two(a):
    high = a.astype(BF16)
    return high, (a - high.astype(F32)).astype(BF16)


def exchange_kernel(
    nx,
    ny,
    nz,
    *refs,
):
    sources, refs = refs[:11], refs[11:]
    body_of_exchange(nx, ny, nz, sources, *refs)


def body_of_exchange(
    nx,
    ny,
    nz,
    sources,
    x_out,
    q_out,
    h_ref,
    head_ref,
    loss_ref,
    wheadt_ref,
    resid_ref,
    attn_ref,
    gain_ref,
    w_both,
    w_down,
    w_head_ref,
    actions_ref,
    step_ref,
    trace_ref,
    targets_ref,
    xs,
    x_mat,
    sel,
    zsum,
    meta,
    meta2,
    gpart,
    grecv,
    gfull,
    hpart,
    psum,
    rs_send,
    rs_recv,
    q_all,
    q_scaled,
    vsum,
    vsum2,
    zcoef,
    hd_part,
    hd_recv,
    hd_y,
    hd_full,
    send_sem,
    recv_sem,
    local_sem,
):
    i = lax.axis_index("dp")
    z = lax.axis_index("ffn")
    core = i % 2
    y = (i // 2) % ny
    x = i // (2 * ny)
    own, depth = resid_ref.shape
    hidden = w_down.shape[0]
    fp = q_all.shape[1]
    half = nz // 2
    tokens = own * nx * ny * 2
    chunk = tokens // nz
    share = own // nz
    bands = 16 // share
    band = depth // bands
    acts = w_head_ref.shape[0]

    def at_x(k):
        return (((x + k) % nx * ny + y) * 2 + core, z)

    def at_y(k):
        return ((x * ny + (y + k) % ny) * 2 + core, z)

    def at_xy(kx, ky):
        return (((x + kx) % nx * ny + (y + ky) % ny) * 2 + core, z)

    def at_z(k):
        return (i, (z + k) % nz)

    sibling = ((x * ny + y) * 2 + 1 - core, z)

    next_sem = [0]
    sends = []

    def copy_pair(src, dst, landing, device):
        n = next_sem[0]
        next_sem[0] += 1
        out = pltpu.make_async_remote_copy(
            src_ref=src,
            dst_ref=dst,
            send_sem=send_sem.at[n],
            recv_sem=recv_sem.at[n],
            device_id=device,
            device_id_type=MESH,
        )
        into = pltpu.make_async_remote_copy(
            src_ref=landing,
            dst_ref=landing,
            send_sem=send_sem.at[n],
            recv_sem=recv_sem.at[n],
            device_id=device,
            device_id_type=MESH,
        )
        sends.append(out)
        return out, into

    def spread(slots, me, n, at):
        arrivals = []
        for k in range(1, n):
            out, into = copy_pair(slots.at[me], slots.at[me], slots.at[(me + n - k) % n], at(k))
            out.start()
            arrivals.append(into)
        return arrivals

    def land(arrivals):
        for into in arrivals:
            into.wait_recv()

    group = 2 * x + core

    def mates():
        for k in range(nx):
            for flip in (0, 1):
                if k or flip:
                    other = core + flip - 2 * core * flip
                    device = (((x + k) % nx * ny + y) * 2 + other, z)
                    yield device, (x + k) % nx * 2 + other, (x + nx - k) % nx * 2 + other

    def spread_row(slots):
        arrivals = []
        for device, _, source in mates():
            out, into = copy_pair(slots.at[group], slots.at[group], slots.at[source], device)
            out.start()
            arrivals.append(into)
        return arrivals

    def total(slots, n):
        result = slots[0]
        for k in range(1, n):
            result = result + slots[k]
        return result

    peers = [device for device, _, _ in mates()] + [at_z(k) for k in range(1, nz)]
    peers += [at_xy(kx, ky) for kx in range(nx) for ky in range(1, ny)]
    barrier = pltpu.get_barrier_semaphore()
    for peer in peers:
        pl.semaphore_signal(barrier, inc=1, device_id=peer, device_id_type=MESH)

    places = (
        resid_ref,
        attn_ref,
        gain_ref,
        w_both.at[0],
        w_both.at[1],
        w_down,
        w_head_ref,
        actions_ref,
        step_ref,
        trace_ref,
        targets_ref,
    )
    loads = [
        pltpu.make_async_copy(src, dst, local_sem.at[n])
        for n, (src, dst) in enumerate(zip(sources, places))
    ]
    for n in (0, 1, 6, 7, 8, 9, 10, 2, 3, 4, 5):
        loads[n].start()

    row = lax.broadcasted_iota(jnp.int32, (own, chunk), 0)
    lane = lax.broadcasted_iota(jnp.int32, (own, chunk), 1)
    row8 = lax.broadcasted_iota(jnp.int32, (8, chunk), 0)
    action_row = lax.broadcasted_iota(jnp.int32, (ROWS, chunk), 0).astype(F32)

    def lanes_of(column):
        return jnp.sum(jnp.where(lane % own == row, column, 0.0), axis=0, keepdims=True)

    def rows_of(vector):
        return jnp.sum(jnp.where(lane == row, vector, 0.0), axis=1, keepdims=True)

    def column_of(vector):
        same = lane[:, :own] == row[:, :own]
        return jnp.sum(jnp.where(same, vector, 0.0), axis=1, keepdims=True)

    def stack(*vectors):
        block = jnp.zeros((8, chunk), F32)
        for n, vector in enumerate(vectors):
            block = jnp.where(row8 == n, vector, block)
        return block

    for n in (0, 1, 6, 7, 8, 9, 10, 2):
        loads[n].wait()
    cuts = nz // 4
    width = gpart.shape[2]

    def put_pieces(pieces, value):
        for p in range(nz):
            r, c = p // cuts, p % cuts
            pieces[p] = value[8 * r : 8 * r + 8, c * width : (c + 1) * width]

    def reduce_start(part, recv):
        arrivals = []
        for k in range(1, nz):
            out, into = copy_pair(
                part.at[(z + k) % nz], recv.at[z], recv.at[(z + nz - k) % nz], at_z(k)
            )
            out.start()
            arrivals.append(into)
        return arrivals

    def reduce_middle(arrivals, part, recv, full):
        recv[z] = part[z]
        land(arrivals)
        full[z] = total(recv, nz)
        return spread(full, z, nz, at_z)

    def pieces_of(full):
        rows = [
            jnp.concatenate([full[r * cuts + c] for c in range(cuts)], axis=1) for r in range(4)
        ]
        return jnp.concatenate(rows, axis=0)

    def wide(value):
        return jnp.concatenate(
            [value, jnp.zeros((ROWS, cuts * width - value.shape[1]), F32)], axis=1
        )

    summed = resid_ref[...].astype(F32) + attn_ref[...].astype(F32)
    squares = jnp.sum(summed * summed, axis=1, keepdims=True)
    eye_acts = (
        lax.broadcasted_iota(jnp.int32, (ROWS, acts), 0)
        == lax.broadcasted_iota(jnp.int32, (ROWS, acts), 1)
    ).astype(BF16)
    w_head_t = dot(eye_acts, w_head_ref[...]).astype(BF16)
    action_own = column_of(actions_ref[...].astype(F32))
    weight_own = column_of(
        jnp.power(jnp.float32(0.97), step_ref[...].astype(F32)) * trace_ref[...].astype(F32) / LEVELS
    )
    target_own = column_of(targets_ref[...])
    one_hot_own = lax.broadcasted_iota(jnp.int32, (own, ROWS), 1).astype(F32) == action_own
    scores = dot(resid_ref[...], w_head_t, NT) + dot(attn_ref[...], w_head_t, NT)
    score = jnp.sum(jnp.where(one_hot_own, scores, 0.0), axis=1, keepdims=True)
    zsum[z] = stack(lanes_of(squares), lanes_of(score))

    pl.semaphore_wait(barrier, len(peers))
    zsum_in = spread(zsum, z, nz, at_z)

    loads[5].wait()
    put_pieces(gpart, wide(dot(w_head_t, w_down[...], NT)))
    g_in = reduce_start(gpart, grecv)
    wheadt_ref[...] = w_head_t

    count = nz * 16
    line = lax.broadcasted_iota(jnp.int32, (count, own), 0)
    place = line // 16
    even = half - place // 2
    offset = jnp.where(place % 2 == 0, -even, half - (place + 1) // 2)
    token = (z + offset + nz) % nz * share + line % share
    token_at = lax.broadcasted_iota(jnp.int32, (count, own), 1) == token
    picks = [(token_at & (line % 16 // share == g)).astype(BF16) for g in range(bands)]

    land(zsum_in)
    zboth = total(zsum, nz)
    mean = rows_of(zboth[0:1]) / (depth * nz)
    normed = (summed * lax.rsqrt(mean + 1e-06) * gain_ref[...]).astype(BF16)

    packed = jnp.zeros((count, band), F32)
    for g in range(bands):
        packed = packed + dot(picks[g], normed[:, g * band : (g + 1) * band])
    chip = x * ny + y
    xs[chip, core] = packed.astype(BF16).reshape(nz, 16, band)

    groups = ((0, 1), (1, 1 + half), (1 + half, nz))
    near_first = lambda n: sorted(range(n), key=lambda k: min(k, n - k))
    coming, third = {}, {}

    def send_group(n):
        places = pl.ds(groups[n][0], groups[n][1] - groups[n][0])
        coming[n] = []
        mine = xs.at[chip, core, places]
        for kx in near_first(nx):
            for ky in near_first(ny):
                if kx or ky:
                    source = (x + nx - kx) % nx * ny + (y + ny - ky) % ny
                    out, into = copy_pair(mine, mine, xs.at[source, core, places], at_xy(kx, ky))
                    out.start()
                    coming[n].append(into)

    def pass_group(n):
        places = pl.ds(groups[n][0], groups[n][1] - groups[n][0])
        land(coming[n])
        mine = xs.at[:, core, places]
        out, third[n] = copy_pair(mine, mine, xs.at[:, 1 - core, places], sibling)
        out.start()

    def gather(r):
        rows = xs[:, :, r].reshape(16 * chunk // share, band)
        for g in range(bands):
            x_mat[r, :, g * band : (g + 1) * band] = dot(sel[g], rows).astype(BF16)

    send_group(0)
    send_group(1)
    psum[...] = jnp.zeros_like(psum)
    to = lax.broadcasted_iota(jnp.int32, (chunk, 16 * chunk // share), 0)
    come = lax.broadcasted_iota(jnp.int32, (chunk, 16 * chunk // share), 1)
    for g in range(bands):
        sel[g] = (come == to // share * 16 + g * share + to % share).astype(BF16)

    here = (row == share * z + lane % share) & (lane // share == i)

    def chunk_of(column):
        return jnp.sum(jnp.where(here, column, 0.0), axis=0, keepdims=True)

    base = rows_of(zboth[1:2]) - target_own
    meta[group] = stack(chunk_of(base), chunk_of(weight_own), chunk_of(action_own))
    meta_in = spread_row(meta)

    pass_group(0)
    send_group(2)
    third[0].wait_recv()

    hops = {(d, h): half if d == h else half - 1 for d in (0, 1) for h in (0, 1)}
    order = ((0, 0), (1, 1), (0, 1), (1, 0))
    sign = (1, -1)

    def chunk_at(offset):
        return (z + nz + offset) % nz

    loads[3].wait()
    loads[4].wait()
    waiting = {}
    cut = -(-fp // 32) * 16
    parts = (slice(0, cut), slice(cut, fp))
    for o in range(half, 0, -1):
        chosen = [dh for dh in order if hops[dh] >= o]
        if o == half - 1:
            third[1].wait_recv()
        if o == half // 2 - 1:
            third[2].wait_recv()
        if o < half:
            gather(2 * (half - o) - 1)
        gather(2 * (half - o))
        for d in (0, 1):
            r = 2 * (half - o) - 1 if d == 0 and o < half else 2 * (half - o)
            for h in (0, 1):
                if (d, h) in chosen:
                    psum[d, h, :hidden] = dot(w_both[h], x_mat[r], NT)
        for p, rows in enumerate(parts):
            for d, h in chosen:
                s = hops[d, h] - o
                value = psum[d, h, rows]
                if s > 0:
                    waiting[d, h, p].wait_recv()
                    value = value + rs_recv[d, h, s - 1, rows].astype(F32)
                rs_send[d, h, s, rows] = value.astype(BF16)
                landing = rs_recv.at[d, h, s, rows]
                out, into = copy_pair(
                    rs_send.at[d, h, s, rows], landing, landing, at_z(sign[d] % nz)
                )
                out.start()
                waiting[d, h, p] = into
            if o == half and p == 0:
                land(meta_in)
                meta2[y] = total(meta, 2 * nx)
                meta_in = spread(meta2, y, ny, at_y)
                g_in = reduce_middle(g_in, gpart, grecv, gfull)
                pass_group(1)

        if o == half - 1:
            pass_group(2)

    if half < 4:
        third[2].wait_recv()
    gather(nz - 1)
    for h in (0, 1):
        psum[0, h, :hidden] = dot(w_both[h], x_mat[nz - 1], NT)
    land(meta_in)
    info = total(meta2, ny)
    land(g_in)
    g_full = jnp.transpose(pieces_of(gfull))[:fp]
    one_hot = (action_row == info[2:3]).astype(BF16)
    g_high, g_low = two(g_full)
    picked_g = dot(g_high, one_hot) + dot(g_low, one_hot)

    lanes = pl.ds(pl.multiple_of(z * chunk, chunk), chunk)
    arriving = {}

    def pass_q(d, h, s, p):
        def piece(c):
            return q_all.at[h, parts[p], pl.ds(pl.multiple_of(c * chunk, chunk), chunk)]

        if s > 0:
            arriving[d, h, p].wait_recv()
        mine = piece(chunk_at(-sign[d] * s))
        out, into = copy_pair(
            mine, mine, piece(chunk_at(-sign[d] * (s + 1))), at_z(sign[d] % nz)
        )
        out.start()
        arriving[d, h, p] = into

    def pass_on(s, p):
        for d, h in order:
            if hops[d, h] > s:
                pass_q(d, h, s, p)

    acts_of = []
    v = jnp.zeros((1, chunk), F32)
    for p, rows in enumerate(parts):
        sums = []
        for h in (0, 1):
            value = psum[0, h, rows]
            for d in (h, 1 - h):
                waiting[d, h, p].wait_recv()
                value = value + rs_recv[d, h, hops[d, h] - 1, rows].astype(F32)
            sums.append(value)
        gate, up = sums
        sg = 1.0 / (1.0 + jnp.exp(-gate))
        silu = gate * sg
        part_g = picked_g[rows]
        q_all[0, rows, lanes] = (part_g * up * sg * (1.0 + gate * (1.0 - sg))).astype(BF16)
        q_all[1, rows, lanes] = (part_g * silu).astype(BF16)
        act = (silu * up).astype(BF16).astype(F32)
        acts_of.append(act)
        v = v + jnp.sum(act * part_g, axis=0, keepdims=True)
        if p == 0:
            pass_on(0, 0)

    vsum[group] = stack(v)
    v_in = spread_row(vsum)
    pass_on(0, 1)
    act = jnp.concatenate(acts_of, axis=0)
    out_copies = []
    for r in range(nz):
        c = chunk_at(-(half - r // 2) if r % 2 == 0 else half - (r + 1) // 2)
        out = pltpu.make_async_copy(x_mat.at[r], x_out.at[c], local_sem.at[11 + r])
        out.start()
        out_copies.append(out)
    pass_on(1, 0)
    land(v_in)
    vsum2[y] = total(vsum, 2 * nx)
    v_in = spread(vsum2, y, ny, at_y)
    pass_on(1, 1)
    land(v_in)
    v_all = total(vsum2, ny)
    differ = info[0:1] + v_all[0:1]
    weight = info[1:2]
    coef = weight * differ

    fl = cuts * width
    strips = fl // 128
    row16 = lax.broadcasted_iota(jnp.int32, (16, 128), 0)
    row16_wide = lax.broadcasted_iota(jnp.int32, (16, fl), 0)

    def put_h(value):
        hpart[z, :, :fl] = value[:16].astype(BF16)
        beside = jnp.zeros((16, 128), F32)
        for n in range((acts - 16) * strips):
            a, k = 16 + n // strips, n % strips
            strip = value[a : a + 1, 128 * k : 128 * k + 128]
            beside = jnp.where(row16 == n, strip, beside)
        hpart[z, :, fl:] = beside.astype(BF16)

    def sum_h():
        value = hpart[0].astype(F32)
        for k in range(1, nz):
            value = value + hpart[k].astype(F32)
        last = jnp.zeros((16, fl), F32)
        for a in range(acts - 16):
            strip = [value[a * strips + k : a * strips + k + 1, fl:] for k in range(strips)]
            last = jnp.where(row16_wide == a, jnp.concatenate(strip, axis=1), last)
        return jnp.concatenate([value[:, :fl], last], axis=0)

    act_high, act_low = two(act * coef)
    put_h(wide(dot(one_hot, act_high, NT) + dot(one_hot, act_low, NT)))
    h_in = spread(hpart, z, nz, at_z)
    zcoef[z] = stack(coef, info[2:3], weight * differ * differ)
    zcoef_in = spread(zcoef, z, nz, at_z)
    for p in (0, 1):
        if half > 2:
            pass_on(2, p)

    land(zcoef_in)
    coef_own = jnp.zeros((own, chunk), F32)
    for c in range(nz):
        mine = (row // share == c) & (lane == i * share + row % share)
        coef_own = jnp.where(mine, zcoef[c, 0:1], coef_own)
    coef_own = jnp.sum(coef_own, axis=1, keepdims=True)
    coef_lanes = jnp.sum(
        jnp.where(lane[:, :own] == row[:, :own], coef_own, 0.0), axis=0, keepdims=True
    )
    picked = jnp.where(
        action_row[:, :own] == actions_ref[...].astype(F32), coef_lanes, 0.0
    )
    p_high, p_low = two(picked)
    head = jnp.zeros((ROWS, depth), F32)
    for ref in (resid_ref, attn_ref):
        head = head + dot(p_high, ref[...]) + dot(p_low, ref[...])
    land(h_in)
    h_sum = sum_h()
    h_high, h_low = two(h_sum[:, :hidden])
    head = head + dot(h_high, w_down[...]) + dot(h_low, w_down[...])
    head_rows, piece = hd_part.shape[1:]
    for g in range(2 * nx):
        hd_part[g] = head[:head_rows, g * piece : (g + 1) * piece]
    hd_recv[group] = hd_part[group]
    hd_in = []
    for device, target, source in mates():
        out, into = copy_pair(hd_part.at[target], hd_recv.at[group], hd_recv.at[source], device)
        out.start()
        hd_in.append(into)

    def scale(c, n):
        lanes = pl.ds(pl.multiple_of(c * chunk, chunk), chunk)
        q_scaled[:, :, lanes] = (q_all[:, :, lanes].astype(F32) * zcoef[c, 0:1]).astype(BF16)
        out = pltpu.make_async_copy(
            q_scaled.at[:, :, lanes], q_out.at[:, :, lanes], local_sem.at[11 + nz + n]
        )
        out.start()
        out_copies.append(out)

    if half > 3:
        pass_on(3, 0)
    scale(z, 0)
    land(hd_in)
    hd_y[y] = total(hd_recv, 2 * nx)
    hd_in = spread(hd_y, y, ny, at_y)
    if half > 3:
        pass_on(3, 1)
    n = 1
    if half > 2:
        scale(chunk_at(1), n)
        scale(chunk_at(-1), n + 1)
        n += 2
    land(hd_in)
    hd_full[group] = total(hd_y, ny)
    hd_in = spread_row(hd_full)
    for o in range(2, half - 1):
        scale(chunk_at(o), n)
        scale(chunk_at(-o), n + 1)
        n += 2
    h_ref[...] = jnp.transpose(h_sum)
    loss = 0.5 * jnp.sum(total(zcoef, nz)[2:3], axis=1, keepdims=True) / tokens
    loss_ref[...] = jnp.broadcast_to(loss, (8, chunk))
    for d, h in order[2:]:
        for p in (0, 1):
            arriving[d, h, p].wait_recv()
    scale(chunk_at(half - 1), n)
    scale(chunk_at(1 - half), n + 1)
    for d, h in order[:2]:
        for p in (0, 1):
            arriving[d, h, p].wait_recv()
    scale(chunk_at(half), n + 2)
    land(hd_in)
    head_ref[...] = jnp.concatenate([hd_full[g] for g in range(2 * nx)], axis=1)
    for out in sends:
        out.wait_send()
    for out in out_copies:
        out.wait()


def grads_kernel(x_ref, q_ref, h_ref, head_ref, loss_ref, wheadt_ref, gg, gu, gd, gh, loss):
    hidden, acts = gd.shape[0], gh.shape[0]
    fp = q_ref.shape[1]
    block = x_ref[...]
    gg[...] = dot(q_ref[0], block)[:hidden]
    gu[...] = dot(q_ref[1], block)[:hidden]
    h_high, h_low = two(h_ref[:fp])
    head_t = wheadt_ref[...]
    gd[...] = (dot(h_high, head_t) + dot(h_low, head_t))[:hidden]
    gh[...] = head_ref[:acts]
    loss[0, 0] = loss_ref[0, 0]


def body(
    nx,
    ny,
    nz,
    resid,
    attn_out,
    norm_gain,
    w_gate,
    w_up,
    w_down,
    w_head,
    actions,
    step_index,
    trace_code,
    targets,
):
    own, depth = resid.shape
    hidden = w_down.shape[0]
    acts = w_head.shape[1]
    fp = -(-hidden // 16) * 16
    fl = -(-hidden // 128) * 128
    tokens = own * nx * ny * 2
    chunk = tokens // nz
    share = own // nz
    bands = 16 // share
    half = nz // 2
    cuts = nz // 4
    head_rows = -(-acts // 8) * 8
    vmem = pl.BlockSpec(memory_space=pltpu.VMEM)
    anywhere = pl.BlockSpec(memory_space=pl.ANY)
    shape = jax.ShapeDtypeStruct
    n_sems = (
        3 * nx * ny + 4 * (2 * nx - 1) + 3 * (ny - 1)
        + 5 * (nz - 1)
        + 4 * 2 * (2 * half - 1)
    )
    pieces = pltpu.VMEM((nz, 8, fl // cuts), F32)
    row_slots = pltpu.VMEM((2 * nx, 8, chunk), F32)
    y_slots = pltpu.VMEM((ny, 8, chunk), F32)
    head_row = pltpu.VMEM((2 * nx, head_rows, depth // (2 * nx)), F32)
    x_out, q, h, head, loss, w_head_t = pl.pallas_call(
        functools.partial(exchange_kernel, nx, ny, nz),
        out_shape=(
            shape((nz, chunk, depth), BF16),
            shape((2, fp, tokens), BF16),
            shape((fl, ROWS), F32),
            shape((head_rows, depth), F32),
            shape((8, chunk), F32),
            shape((ROWS, depth), BF16),
        ),
        in_specs=[pl.BlockSpec(memory_space=pltpu.HBM)] * 11,
        out_specs=(anywhere, anywhere, vmem, vmem, vmem, vmem),
        scratch_shapes=[
            pltpu.VMEM((own, depth), BF16),
            pltpu.VMEM((own, depth), BF16),
            pltpu.VMEM((1, depth), F32),
            pltpu.VMEM((2, hidden, depth), BF16),
            pltpu.VMEM((hidden, depth), BF16),
            pltpu.VMEM((acts, depth), BF16),
            pltpu.VMEM((1, own), jnp.int32),
            pltpu.VMEM((1, own), jnp.int32),
            pltpu.VMEM((1, own), jnp.int32),
            pltpu.VMEM((1, own), F32),
            pltpu.VMEM((nx * ny, 2, nz, 16, depth // bands), BF16),
            pltpu.VMEM((nz, chunk, depth), BF16),
            pltpu.VMEM((bands, chunk, 16 * chunk // share), BF16),
            pltpu.VMEM((nz, 8, chunk), F32),
            row_slots,
            y_slots,
            pieces,
            pieces,
            pieces,
            pltpu.VMEM((nz, 16, fl + 128), BF16),
            pltpu.VMEM((2, 2, fp, chunk), F32),
            pltpu.VMEM((2, 2, half, fp, chunk), BF16),
            pltpu.VMEM((2, 2, half, fp, chunk), BF16),
            pltpu.VMEM((2, fp, tokens), BF16),
            pltpu.VMEM((2, fp, tokens), BF16),
            row_slots,
            y_slots,
            pltpu.VMEM((nz, 8, chunk), F32),
            head_row,
            head_row,
            pltpu.VMEM((ny, head_rows, depth // (2 * nx)), F32),
            head_row,
            pltpu.SemaphoreType.DMA((n_sems,)),
            pltpu.SemaphoreType.DMA((n_sems,)),
            pltpu.SemaphoreType.DMA((11 + 2 * nz,)),
        ],
        compiler_params=pltpu.CompilerParams(
            collective_id=0, has_side_effects=True, vmem_limit_bytes=60 * 1024 * 1024
        ),
        name="exchange",
    )(
        resid,
        attn_out,
        norm_gain.reshape(1, depth),
        w_gate.T,
        w_up.T,
        w_down,
        w_head.T,
        actions.reshape(1, own),
        step_index.reshape(1, own),
        trace_code.reshape(1, own),
        targets.reshape(1, own),
    )

    tile = min(256, depth)
    grad_gate, grad_up, grad_down, grad_head, loss = pl.pallas_call(
        grads_kernel,
        grid=(depth // tile,),
        out_shape=(
            shape((hidden, depth), F32),
            shape((hidden, depth), F32),
            shape((hidden, depth), F32),
            shape((acts, depth), F32),
            shape((1, 1), F32),
        ),
        in_specs=[
            pl.BlockSpec((tokens, tile), lambda n: (0, n)),
            pl.BlockSpec((2, fp, tokens), lambda n: (0, 0, 0)),
            pl.BlockSpec((fl, ROWS), lambda n: (0, 0)),
            pl.BlockSpec((head_rows, tile), lambda n: (0, n)),
            pl.BlockSpec((8, chunk), lambda n: (0, 0)),
            pl.BlockSpec((ROWS, tile), lambda n: (0, n)),
        ],
        out_specs=(
            pl.BlockSpec((hidden, tile), lambda n: (0, n)),
            pl.BlockSpec((hidden, tile), lambda n: (0, n)),
            pl.BlockSpec((hidden, tile), lambda n: (0, n)),
            pl.BlockSpec((acts, tile), lambda n: (0, n)),
            pl.BlockSpec((1, 1), lambda n: (0, 0), memory_space=pltpu.SMEM),
        ),
        compiler_params=pltpu.CompilerParams(vmem_limit_bytes=60 * 1024 * 1024),
        name="weight_grads",
    )(x_out.reshape(tokens, depth), q, h, head, loss, w_head_t)
    return grad_gate.T, grad_up.T, grad_down, grad_head.T, loss.reshape(())


def build(mesh, nx, ny):
    nz = mesh.shape["ffn"]
    in_specs = (
        P("dp", "ffn"),
        P("dp", "ffn"),
        P("ffn"),
        P("ffn", "dp"),
        P("ffn", "dp"),
        P("dp", "ffn"),
        P("ffn", None),
        P("dp"),
        P("dp"),
        P("dp"),
        P("dp"),
    )
    out_specs = (P("ffn", "dp"), P("ffn", "dp"), P("dp", "ffn"), P("ffn", None), P())
    return jax.shard_map(
        functools.partial(body, nx, ny, nz),
        mesh=mesh,
        in_specs=in_specs,
        out_specs=out_specs,
        check_vma=False,
    )


def solution(mesh):
    return build(mesh, 4, 4)
```

```python
import functools

import jax
import jax.numpy as jnp
from jax import lax
from jax.experimental import pallas as pl
from jax.experimental.pallas import tpu as pltpu
from jax.sharding import PartitionSpec as P

MESH = pl.DeviceIdType.MESH
F32 = jnp.float32
BF16 = jnp.bfloat16
LEVELS = 8
ROWS = 32
NT = (((1,), (1,)), ((), ()))
NN = (((1,), (0,)), ((), ()))


def dot(a, b, dims=NN):
    return lax.dot_general(a, b, dims, preferred_element_type=F32)


def two(a):
    high = a.astype(BF16)
    return high, (a - high.astype(F32)).astype(BF16)


def exchange_kernel(
    nx,
    ny,
    nz,
    *refs,
):
    sources, refs = refs[:11], refs[11:]
    body_of_exchange(nx, ny, nz, sources, *refs)


def body_of_exchange(
    nx,
    ny,
    nz,
    sources,
    x_out,
    q_out,
    h_ref,
    head_ref,
    loss_ref,
    wheadt_ref,
    resid_ref,
    attn_ref,
    gain_ref,
    w_both,
    w_down,
    w_head_ref,
    actions_ref,
    step_ref,
    trace_ref,
    targets_ref,
    xs,
    x_mat,
    sel,
    zsum,
    meta,
    meta2,
    gpart,
    grecv,
    gfull,
    hpart,
    psum,
    rs_send,
    rs_recv,
    q_all,
    q_scaled,
    vsum,
    vsum2,
    zcoef,
    hd_part,
    hd_recv,
    hd_y,
    hd_full,
    send_sem,
    recv_sem,
    local_sem,
):
    i = lax.axis_index("dp")
    z = lax.axis_index("ffn")
    core = i % 2
    y = (i // 2) % ny
    x = i // (2 * ny)
    own, depth = resid_ref.shape
    hidden = w_down.shape[0]
    fp = q_all.shape[1]
    half = nz // 2
    tokens = own * nx * ny * 2
    chunk = tokens // nz
    share = own // nz
    bands = 16 // share
    band = depth // bands
    acts = w_head_ref.shape[0]

    def at_x(k):
        return (((x + k) % nx * ny + y) * 2 + core, z)

    def at_y(k):
        return ((x * ny + (y + k) % ny) * 2 + core, z)

    def at_xy(kx, ky):
        return (((x + kx) % nx * ny + (y + ky) % ny) * 2 + core, z)

    def at_z(k):
        return (i, (z + k) % nz)

    sibling = ((x * ny + y) * 2 + 1 - core, z)

    next_sem = [0]
    sends = []

    def copy_pair(src, dst, landing, device):
        n = next_sem[0]
        next_sem[0] += 1
        out = pltpu.make_async_remote_copy(
            src_ref=src,
            dst_ref=dst,
            send_sem=send_sem.at[n],
            recv_sem=recv_sem.at[n],
            device_id=device,
            device_id_type=MESH,
        )
        into = pltpu.make_async_remote_copy(
            src_ref=landing,
            dst_ref=landing,
            send_sem=send_sem.at[n],
            recv_sem=recv_sem.at[n],
            device_id=device,
            device_id_type=MESH,
        )
        sends.append(out)
        return out, into

    def spread(slots, me, n, at):
        arrivals = []
        for k in range(1, n):
            out, into = copy_pair(slots.at[me], slots.at[me], slots.at[(me + n - k) % n], at(k))
            out.start()
            arrivals.append(into)
        return arrivals

    def land(arrivals):
        for into in arrivals:
            into.wait_recv()

    group = 2 * x + core

    def mates():
        for k in range(nx):
            for flip in (0, 1):
                if k or flip:
                    other = core + flip - 2 * core * flip
                    device = (((x + k) % nx * ny + y) * 2 + other, z)
                    yield device, (x + k) % nx * 2 + other, (x + nx - k) % nx * 2 + other

    def spread_row(slots):
        arrivals = []
        for device, _, source in mates():
            out, into = copy_pair(slots.at[group], slots.at[group], slots.at[source], device)
            out.start()
            arrivals.append(into)
        return arrivals

    def total(slots, n):
        result = slots[0]
        for k in range(1, n):
            result = result + slots[k]
        return result

    peers = [device for device, _, _ in mates()] + [at_z(k) for k in range(1, nz)]
    peers += [at_xy(kx, ky) for kx in range(nx) for ky in range(1, ny)]
    barrier = pltpu.get_barrier_semaphore()
    for peer in peers:
        pl.semaphore_signal(barrier, inc=1, device_id=peer, device_id_type=MESH)

    places = (
        resid_ref,
        attn_ref,
        gain_ref,
        w_both.at[0],
        w_both.at[1],
        w_down,
        w_head_ref,
        actions_ref,
        step_ref,
        trace_ref,
        targets_ref,
    )
    loads = [
        pltpu.make_async_copy(src, dst, local_sem.at[n])
        for n, (src, dst) in enumerate(zip(sources, places))
    ]
    for n in (0, 1, 6, 7, 8, 9, 10, 2, 3, 4, 5):
        loads[n].start()

    row = lax.broadcasted_iota(jnp.int32, (own, chunk), 0)
    lane = lax.broadcasted_iota(jnp.int32, (own, chunk), 1)
    row8 = lax.broadcasted_iota(jnp.int32, (8, chunk), 0)
    action_row = lax.broadcasted_iota(jnp.int32, (ROWS, chunk), 0).astype(F32)

    def lanes_of(column):
        return jnp.sum(jnp.where(lane % own == row, column, 0.0), axis=0, keepdims=True)

    def rows_of(vector):
        return jnp.sum(jnp.where(lane == row, vector, 0.0), axis=1, keepdims=True)

    def column_of(vector):
        same = lane[:, :own] == row[:, :own]
        return jnp.sum(jnp.where(same, vector, 0.0), axis=1, keepdims=True)

    def stack(*vectors):
        block = jnp.zeros((8, chunk), F32)
        for n, vector in enumerate(vectors):
            block = jnp.where(row8 == n, vector, block)
        return block

    for n in (0, 1, 6, 7, 8, 9, 10, 2):
        loads[n].wait()
    cuts = nz // 4
    width = gpart.shape[2]

    def put_pieces(pieces, value):
        for p in range(nz):
            r, c = p // cuts, p % cuts
            pieces[p] = value[8 * r : 8 * r + 8, c * width : (c + 1) * width]

    def reduce_start(part, recv):
        arrivals = []
        for k in range(1, nz):
            out, into = copy_pair(
                part.at[(z + k) % nz], recv.at[z], recv.at[(z + nz - k) % nz], at_z(k)
            )
            out.start()
            arrivals.append(into)
        return arrivals

    def reduce_middle(arrivals, part, recv, full):
        recv[z] = part[z]
        land(arrivals)
        full[z] = total(recv, nz)
        return spread(full, z, nz, at_z)

    def pieces_of(full):
        rows = [
            jnp.concatenate([full[r * cuts + c] for c in range(cuts)], axis=1) for r in range(4)
        ]
        return jnp.concatenate(rows, axis=0)

    def wide(value):
        return jnp.concatenate(
            [value, jnp.zeros((ROWS, cuts * width - value.shape[1]), F32)], axis=1
        )

    summed = resid_ref[...].astype(F32) + attn_ref[...].astype(F32)
    squares = jnp.sum(summed * summed, axis=1, keepdims=True)
    eye_acts = (
        lax.broadcasted_iota(jnp.int32, (ROWS, acts), 0)
        == lax.broadcasted_iota(jnp.int32, (ROWS, acts), 1)
    ).astype(BF16)
    w_head_t = dot(eye_acts, w_head_ref[...]).astype(BF16)
    action_own = column_of(actions_ref[...].astype(F32))
    weight_own = column_of(
        jnp.power(jnp.float32(0.97), step_ref[...].astype(F32)) * trace_ref[...].astype(F32) / LEVELS
    )
    target_own = column_of(targets_ref[...])
    one_hot_own = lax.broadcasted_iota(jnp.int32, (own, ROWS), 1).astype(F32) == action_own
    scores = dot(resid_ref[...], w_head_t, NT) + dot(attn_ref[...], w_head_t, NT)
    score = jnp.sum(jnp.where(one_hot_own, scores, 0.0), axis=1, keepdims=True)
    zsum[z] = stack(lanes_of(squares), lanes_of(score))

    pl.semaphore_wait(barrier, len(peers))
    zsum_in = spread(zsum, z, nz, at_z)

    loads[5].wait()
    put_pieces(gpart, wide(dot(w_head_t, w_down[...], NT)))
    g_in = reduce_start(gpart, grecv)
    wheadt_ref[...] = w_head_t

    count = nz * 16
    line = lax.broadcasted_iota(jnp.int32, (count, own), 0)
    place = line // 16
    even = half - place // 2
    offset = jnp.where(place % 2 == 0, -even, half - (place + 1) // 2)
    token = (z + offset + nz) % nz * share + line % share
    token_at = lax.broadcasted_iota(jnp.int32, (count, own), 1) == token
    picks = [(token_at & (line % 16 // share == g)).astype(BF16) for g in range(bands)]

    land(zsum_in)
    zboth = total(zsum, nz)
    mean = rows_of(zboth[0:1]) / (depth * nz)
    normed = (summed * lax.rsqrt(mean + 1e-06) * gain_ref[...]).astype(BF16)

    packed = jnp.zeros((count, band), F32)
    for g in range(bands):
        packed = packed + dot(picks[g], normed[:, g * band : (g + 1) * band])
    chip = x * ny + y
    xs[chip, core] = packed.astype(BF16).reshape(nz, 16, band)

    groups = ((0, 1), (1, 1 + half), (1 + half, nz))
    near_first = lambda n: sorted(range(n), key=lambda k: min(k, n - k))
    coming, third = {}, {}

    def send_group(n):
        places = pl.ds(groups[n][0], groups[n][1] - groups[n][0])
        coming[n] = []
        mine = xs.at[chip, core, places]
        for kx in near_first(nx):
            for ky in near_first(ny):
                if kx or ky:
                    source = (x + nx - kx) % nx * ny + (y + ny - ky) % ny
                    out, into = copy_pair(mine, mine, xs.at[source, core, places], at_xy(kx, ky))
                    out.start()
                    coming[n].append(into)

    def pass_group(n):
        places = pl.ds(groups[n][0], groups[n][1] - groups[n][0])
        land(coming[n])
        mine = xs.at[:, core, places]
        out, third[n] = copy_pair(mine, mine, xs.at[:, 1 - core, places], sibling)
        out.start()

    def gather(r):
        rows = xs[:, :, r].reshape(16 * chunk // share, band)
        for g in range(bands):
            x_mat[r, :, g * band : (g + 1) * band] = dot(sel[g], rows).astype(BF16)

    send_group(0)
    send_group(1)
    psum[...] = jnp.zeros_like(psum)
    to = lax.broadcasted_iota(jnp.int32, (chunk, 16 * chunk // share), 0)
    come = lax.broadcasted_iota(jnp.int32, (chunk, 16 * chunk // share), 1)
    for g in range(bands):
        sel[g] = (come == to // share * 16 + g * share + to % share).astype(BF16)

    here = (row == share * z + lane % share) & (lane // share == i)

    def chunk_of(column):
        return jnp.sum(jnp.where(here, column, 0.0), axis=0, keepdims=True)

    base = rows_of(zboth[1:2]) - target_own
    meta[group] = stack(chunk_of(base), chunk_of(weight_own), chunk_of(action_own))
    meta_in = spread_row(meta)

    pass_group(0)
    send_group(2)
    third[0].wait_recv()

    hops = {(d, h): half if d == h else half - 1 for d in (0, 1) for h in (0, 1)}
    order = ((0, 0), (1, 1), (0, 1), (1, 0))
    sign = (1, -1)

    def chunk_at(offset):
        return (z + nz + offset) % nz

    loads[3].wait()
    loads[4].wait()
    waiting = {}
    cut = -(-fp // 32) * 16
    parts = (slice(0, cut), slice(cut, fp))
    for o in range(half, 0, -1):
        chosen = [dh for dh in order if hops[dh] >= o]
        if o == half - 1:
            third[1].wait_recv()
        if o == half // 2 - 1:
            third[2].wait_recv()
        if o < half:
            gather(2 * (half - o) - 1)
        gather(2 * (half - o))
        for d in (0, 1):
            r = 2 * (half - o) - 1 if d == 0 and o < half else 2 * (half - o)
            for h in (0, 1):
                if (d, h) in chosen:
                    psum[d, h, :hidden] = dot(w_both[h], x_mat[r], NT)
        for p, rows in enumerate(parts):
            for d, h in chosen:
                s = hops[d, h] - o
                value = psum[d, h, rows]
                if s > 0:
                    waiting[d, h, p].wait_recv()
                    value = value + rs_recv[d, h, s - 1, rows].astype(F32)
                rs_send[d, h, s, rows] = value.astype(BF16)
                landing = rs_recv.at[d, h, s, rows]
                out, into = copy_pair(
                    rs_send.at[d, h, s, rows], landing, landing, at_z(sign[d] % nz)
                )
                out.start()
                waiting[d, h, p] = into
            if o == half and p == 0:
                land(meta_in)
                meta2[y] = total(meta, 2 * nx)
                meta_in = spread(meta2, y, ny, at_y)
                g_in = reduce_middle(g_in, gpart, grecv, gfull)
                pass_group(1)

        if o == half - 1:
            pass_group(2)

    if half < 4:
        third[2].wait_recv()
    gather(nz - 1)
    for h in (0, 1):
        psum[0, h, :hidden] = dot(w_both[h], x_mat[nz - 1], NT)
    land(meta_in)
    info = total(meta2, ny)
    land(g_in)
    g_full = jnp.transpose(pieces_of(gfull))[:fp]
    one_hot = (action_row == info[2:3]).astype(BF16)
    g_high, g_low = two(g_full)
    picked_g = dot(g_high, one_hot) + dot(g_low, one_hot)

    lanes = pl.ds(pl.multiple_of(z * chunk, chunk), chunk)
    arriving = {}

    def pass_q(d, h, s, p):
        def piece(c):
            return q_all.at[h, parts[p], pl.ds(pl.multiple_of(c * chunk, chunk), chunk)]

        if s > 0:
            arriving[d, h, p].wait_recv()
        mine = piece(chunk_at(-sign[d] * s))
        out, into = copy_pair(
            mine, mine, piece(chunk_at(-sign[d] * (s + 1))), at_z(sign[d] % nz)
        )
        out.start()
        arriving[d, h, p] = into

    def pass_on(s, p):
        for d, h in order:
            if hops[d, h] > s:
                pass_q(d, h, s, p)

    acts_of = []
    v = jnp.zeros((1, chunk), F32)
    for p, rows in enumerate(parts):
        sums = []
        for h in (0, 1):
            value = psum[0, h, rows]
            for d in (h, 1 - h):
                waiting[d, h, p].wait_recv()
                value = value + rs_recv[d, h, hops[d, h] - 1, rows].astype(F32)
            sums.append(value)
        gate, up = sums
        sg = 1.0 / (1.0 + jnp.exp(-gate))
        silu = gate * sg
        part_g = picked_g[rows]
        q_all[0, rows, lanes] = (part_g * up * sg * (1.0 + gate * (1.0 - sg))).astype(BF16)
        q_all[1, rows, lanes] = (part_g * silu).astype(BF16)
        act = (silu * up).astype(BF16).astype(F32)
        acts_of.append(act)
        v = v + jnp.sum(act * part_g, axis=0, keepdims=True)
        if p == 0:
            pass_on(0, 0)

    vsum[group] = stack(v)
    v_in = spread_row(vsum)
    pass_on(0, 1)
    act = jnp.concatenate(acts_of, axis=0)
    out_copies = []
    for r in range(nz):
        c = chunk_at(-(half - r // 2) if r % 2 == 0 else half - (r + 1) // 2)
        out = pltpu.make_async_copy(x_mat.at[r], x_out.at[c], local_sem.at[11 + r])
        out.start()
        out_copies.append(out)
    pass_on(1, 0)
    land(v_in)
    vsum2[y] = total(vsum, 2 * nx)
    v_in = spread(vsum2, y, ny, at_y)
    pass_on(1, 1)
    land(v_in)
    v_all = total(vsum2, ny)
    differ = info[0:1] + v_all[0:1]
    weight = info[1:2]
    coef = weight * differ

    fl = cuts * width
    strips = fl // 128
    row16 = lax.broadcasted_iota(jnp.int32, (16, 128), 0)
    row16_wide = lax.broadcasted_iota(jnp.int32, (16, fl), 0)

    def put_h(value):
        hpart[z, :, :fl] = value[:16].astype(BF16)
        beside = jnp.zeros((16, 128), F32)
        for n in range((acts - 16) * strips):
            a, k = 16 + n // strips, n % strips
            strip = value[a : a + 1, 128 * k : 128 * k + 128]
            beside = jnp.where(row16 == n, strip, beside)
        hpart[z, :, fl:] = beside.astype(BF16)

    def sum_h():
        value = hpart[0].astype(F32)
        for k in range(1, nz):
            value = value + hpart[k].astype(F32)
        last = jnp.zeros((16, fl), F32)
        for a in range(acts - 16):
            strip = [value[a * strips + k : a * strips + k + 1, fl:] for k in range(strips)]
            last = jnp.where(row16_wide == a, jnp.concatenate(strip, axis=1), last)
        return jnp.concatenate([value[:, :fl], last], axis=0)

    act_high, act_low = two(act * coef)
    put_h(wide(dot(one_hot, act_high, NT) + dot(one_hot, act_low, NT)))
    h_in = spread(hpart, z, nz, at_z)
    zcoef[z] = stack(coef, info[2:3], weight * differ * differ)
    zcoef_in = spread(zcoef, z, nz, at_z)
    for p in (0, 1):
        if half > 2:
            pass_on(2, p)

    land(zcoef_in)
    coef_own = jnp.zeros((own, chunk), F32)
    for c in range(nz):
        mine = (row // share == c) & (lane == i * share + row % share)
        coef_own = jnp.where(mine, zcoef[c, 0:1], coef_own)
    coef_own = jnp.sum(coef_own, axis=1, keepdims=True)
    coef_lanes = jnp.sum(
        jnp.where(lane[:, :own] == row[:, :own], coef_own, 0.0), axis=0, keepdims=True
    )
    picked = jnp.where(
        action_row[:, :own] == actions_ref[...].astype(F32), coef_lanes, 0.0
    )
    p_high, p_low = two(picked)
    head = jnp.zeros((ROWS, depth), F32)
    for ref in (resid_ref, attn_ref):
        head = head + dot(p_high, ref[...]) + dot(p_low, ref[...])
    land(h_in)
    h_sum = sum_h()
    h_high, h_low = two(h_sum[:, :hidden])
    head = head + dot(h_high, w_down[...]) + dot(h_low, w_down[...])
    head_rows, piece = hd_part.shape[1:]
    for g in range(2 * nx):
        hd_part[g] = head[:head_rows, g * piece : (g + 1) * piece]
    hd_recv[group] = hd_part[group]
    hd_in = []
    for device, target, source in mates():
        out, into = copy_pair(hd_part.at[target], hd_recv.at[group], hd_recv.at[source], device)
        out.start()
        hd_in.append(into)

    def scale(c, n):
        lanes = pl.ds(pl.multiple_of(c * chunk, chunk), chunk)
        q_scaled[:, :, lanes] = (q_all[:, :, lanes].astype(F32) * zcoef[c, 0:1]).astype(BF16)
        out = pltpu.make_async_copy(
            q_scaled.at[:, :, lanes], q_out.at[:, :, lanes], local_sem.at[11 + nz + n]
        )
        out.start()
        out_copies.append(out)

    if half > 3:
        pass_on(3, 0)
    land(hd_in)
    hd_y[y] = total(hd_recv, 2 * nx)
    hd_in = spread(hd_y, y, ny, at_y)
    if half > 3:
        pass_on(3, 1)
    scale(z, 0)
    land(hd_in)
    hd_full[group] = total(hd_y, ny)
    hd_in = spread_row(hd_full)
    n = 1
    if half > 2:
        scale(chunk_at(1), n)
        scale(chunk_at(-1), n + 1)
        n += 2
    for o in range(2, half - 1):
        scale(chunk_at(o), n)
        scale(chunk_at(-o), n + 1)
        n += 2
    h_ref[...] = jnp.transpose(h_sum)
    loss = 0.5 * jnp.sum(total(zcoef, nz)[2:3], axis=1, keepdims=True) / tokens
    loss_ref[...] = jnp.broadcast_to(loss, (8, chunk))
    for d, h in order[2:]:
        for p in (0, 1):
            arriving[d, h, p].wait_recv()
    scale(chunk_at(half - 1), n)
    scale(chunk_at(1 - half), n + 1)
    for d, h in order[:2]:
        for p in (0, 1):
            arriving[d, h, p].wait_recv()
    scale(chunk_at(half), n + 2)
    land(hd_in)
    head_ref[...] = jnp.concatenate([hd_full[g] for g in range(2 * nx)], axis=1)
    for out in sends:
        out.wait_send()
    for out in out_copies:
        out.wait()


def grads_kernel(x_ref, q_ref, h_ref, head_ref, loss_ref, wheadt_ref, gg, gu, gd, gh, loss):
    hidden, acts = gd.shape[0], gh.shape[0]
    fp = q_ref.shape[1]
    block = x_ref[...]
    gg[...] = dot(q_ref[0], block)[:hidden]
    gu[...] = dot(q_ref[1], block)[:hidden]
    h_high, h_low = two(h_ref[:fp])
    head_t = wheadt_ref[...]
    gd[...] = (dot(h_high, head_t) + dot(h_low, head_t))[:hidden]
    gh[...] = head_ref[:acts]
    loss[0, 0] = loss_ref[0, 0]


def body(
    nx,
    ny,
    nz,
    resid,
    attn_out,
    norm_gain,
    w_gate,
    w_up,
    w_down,
    w_head,
    actions,
    step_index,
    trace_code,
    targets,
):
    own, depth = resid.shape
    hidden = w_down.shape[0]
    acts = w_head.shape[1]
    fp = -(-hidden // 16) * 16
    fl = -(-hidden // 128) * 128
    tokens = own * nx * ny * 2
    chunk = tokens // nz
    share = own // nz
    bands = 16 // share
    half = nz // 2
    cuts = nz // 4
    head_rows = -(-acts // 8) * 8
    vmem = pl.BlockSpec(memory_space=pltpu.VMEM)
    anywhere = pl.BlockSpec(memory_space=pl.ANY)
    shape = jax.ShapeDtypeStruct
    n_sems = (
        3 * nx * ny + 4 * (2 * nx - 1) + 3 * (ny - 1)
        + 5 * (nz - 1)
        + 4 * 2 * (2 * half - 1)
    )
    pieces = pltpu.VMEM((nz, 8, fl // cuts), F32)
    row_slots = pltpu.VMEM((2 * nx, 8, chunk), F32)
    y_slots = pltpu.VMEM((ny, 8, chunk), F32)
    head_row = pltpu.VMEM((2 * nx, head_rows, depth // (2 * nx)), F32)
    x_out, q, h, head, loss, w_head_t = pl.pallas_call(
        functools.partial(exchange_kernel, nx, ny, nz),
        out_shape=(
            shape((nz, chunk, depth), BF16),
            shape((2, fp, tokens), BF16),
            shape((fl, ROWS), F32),
            shape((head_rows, depth), F32),
            shape((8, chunk), F32),
            shape((ROWS, depth), BF16),
        ),
        in_specs=[pl.BlockSpec(memory_space=pltpu.HBM)] * 11,
        out_specs=(anywhere, anywhere, vmem, vmem, vmem, vmem),
        scratch_shapes=[
            pltpu.VMEM((own, depth), BF16),
            pltpu.VMEM((own, depth), BF16),
            pltpu.VMEM((1, depth), F32),
            pltpu.VMEM((2, hidden, depth), BF16),
            pltpu.VMEM((hidden, depth), BF16),
            pltpu.VMEM((acts, depth), BF16),
            pltpu.VMEM((1, own), jnp.int32),
            pltpu.VMEM((1, own), jnp.int32),
            pltpu.VMEM((1, own), jnp.int32),
            pltpu.VMEM((1, own), F32),
            pltpu.VMEM((nx * ny, 2, nz, 16, depth // bands), BF16),
            pltpu.VMEM((nz, chunk, depth), BF16),
            pltpu.VMEM((bands, chunk, 16 * chunk // share), BF16),
            pltpu.VMEM((nz, 8, chunk), F32),
            row_slots,
            y_slots,
            pieces,
            pieces,
            pieces,
            pltpu.VMEM((nz, 16, fl + 128), BF16),
            pltpu.VMEM((2, 2, fp, chunk), F32),
            pltpu.VMEM((2, 2, half, fp, chunk), BF16),
            pltpu.VMEM((2, 2, half, fp, chunk), BF16),
            pltpu.VMEM((2, fp, tokens), BF16),
            pltpu.VMEM((2, fp, tokens), BF16),
            row_slots,
            y_slots,
            pltpu.VMEM((nz, 8, chunk), F32),
            head_row,
            head_row,
            pltpu.VMEM((ny, head_rows, depth // (2 * nx)), F32),
            head_row,
            pltpu.SemaphoreType.DMA((n_sems,)),
            pltpu.SemaphoreType.DMA((n_sems,)),
            pltpu.SemaphoreType.DMA((11 + 2 * nz,)),
        ],
        compiler_params=pltpu.CompilerParams(
            collective_id=0, has_side_effects=True, vmem_limit_bytes=60 * 1024 * 1024
        ),
        name="exchange",
    )(
        resid,
        attn_out,
        norm_gain.reshape(1, depth),
        w_gate.T,
        w_up.T,
        w_down,
        w_head.T,
        actions.reshape(1, own),
        step_index.reshape(1, own),
        trace_code.reshape(1, own),
        targets.reshape(1, own),
    )

    tile = min(512, depth)
    grad_gate, grad_up, grad_down, grad_head, loss = pl.pallas_call(
        grads_kernel,
        grid=(depth // tile,),
        out_shape=(
            shape((hidden, depth), F32),
            shape((hidden, depth), F32),
            shape((hidden, depth), F32),
            shape((acts, depth), F32),
            shape((1, 1), F32),
        ),
        in_specs=[
            pl.BlockSpec((tokens, tile), lambda n: (0, n)),
            pl.BlockSpec((2, fp, tokens), lambda n: (0, 0, 0)),
            pl.BlockSpec((fl, ROWS), lambda n: (0, 0)),
            pl.BlockSpec((head_rows, tile), lambda n: (0, n)),
            pl.BlockSpec((8, chunk), lambda n: (0, 0)),
            pl.BlockSpec((ROWS, tile), lambda n: (0, n)),
        ],
        out_specs=(
            pl.BlockSpec((hidden, tile), lambda n: (0, n)),
            pl.BlockSpec((hidden, tile), lambda n: (0, n)),
            pl.BlockSpec((hidden, tile), lambda n: (0, n)),
            pl.BlockSpec((acts, tile), lambda n: (0, n)),
            pl.BlockSpec((1, 1), lambda n: (0, 0), memory_space=pltpu.SMEM),
        ),
        compiler_params=pltpu.CompilerParams(vmem_limit_bytes=60 * 1024 * 1024),
        name="weight_grads",
    )(x_out.reshape(tokens, depth), q, h, head, loss, w_head_t)
    return grad_gate.T, grad_up.T, grad_down, grad_head.T, loss.reshape(())


def build(mesh, nx, ny):
    nz = mesh.shape["ffn"]
    in_specs = (
        P("dp", "ffn"),
        P("dp", "ffn"),
        P("ffn"),
        P("ffn", "dp"),
        P("ffn", "dp"),
        P("dp", "ffn"),
        P("ffn", None),
        P("dp"),
        P("dp"),
        P("dp"),
        P("dp"),
    )
    out_specs = (P("ffn", "dp"), P("ffn", "dp"), P("dp", "ffn"), P("ffn", None), P())
    return jax.shard_map(
        functools.partial(body, nx, ny, nz),
        mesh=mesh,
        in_specs=in_specs,
        out_specs=out_specs,
        check_vma=False,
    )


def solution(mesh):
    return build(mesh, 4, 4)
```
